32 devices in a mesh: seq: 8 (over z, y), tp: 4 (over x, core).
Axes of the slice: x: 2, y: 2, z: 4, core: 2. Of those that a mesh axis runs over, the one named last changes fastest.
Arguments:
- query_rows: bfloat16 [4096, 2560], P(('seq', 'tp')), may hold values from -6 to 6
- key_rows: bfloat16 [4096, 512], P(('seq', 'tp')), may hold values from -6 to 6
- value_rows: bfloat16 [4096, 512], P(('seq', 'tp')), may hold values from -6 to 6
- out_grad: bfloat16 [4096, 2560], P(('seq', 'tp')), may hold values from -6 to 6
- doc_lengths: int32 [8], replicated, may hold values from 1 to 1024, as said below
Outputs:
- attended: bfloat16 [4096, 2560], P(('seq', 'tp'))
- query_grad: bfloat16 [4096, 2560], P(('seq', 'tp'))
- key_grad: bfloat16 [4096, 512], P(('seq', 'tp'))
- value_grad: bfloat16 [4096, 512], P(('seq', 'tp'))
The draws below stay inside these ranges and needn't reach their ends.
Inputs may be any that keep to these rules, and one draw needn't show every extreme that they name: `doc_lengths`: 8 document lengths in token order that sum to 4096; exactly one of them is 1024, all others are shorter.
All inputs are finite; a program needn't handle non-finite values.
Results may differ from the reference program's by a relative error of at most 0.022.
Values may be sent and summed in bfloat16 or wider, within the bound.
A program may use at most 64 MiB of HBM per device.

```python
import math
import jax
import jax.numpy as jnp
from jax import lax

HD = 128
QH = 20
KVH = 4
DOCS = 8
TOKENS = 4096
LONG = 1024


def doc_plan(key):
    base = jax.random.fold_in(key, 11)
    first, second = jax.random.split(base)
    remainder = TOKENS - LONG
    pieces = DOCS - 1
    share = remainder // pieces
    pairs = pieces // 2
    moves = jax.random.randint(first, (pairs,), 1 - share, share).astype(jnp.int32)
    paired = jnp.stack([share + moves, share - moves], axis=1).reshape(2 * pairs)
    shorter = jnp.concatenate([paired, jnp.full((pieces - 2 * pairs,), share, jnp.int32)])
    shorter = shorter.at[pieces - 1].add(remainder - share * pieces)
    long_slot = jax.random.randint(second, (), 0, DOCS)
    ordinal = jnp.arange(DOCS, dtype=jnp.int32)
    source = jnp.clip(ordinal - (ordinal > long_slot).astype(jnp.int32), 0, DOCS - 2)
    lengths = jnp.where(ordinal == long_slot, LONG, shorter[source]).astype(jnp.int32)
    return lengths


def rough_rows(key, shape):
    values_out = jax.random.normal(key, shape, jnp.float32) * 1.6
    return jnp.clip(values_out, -6.0, 6.0)


def draw_doc_lengths(key, part):
    return doc_plan(key)


def draw_key_rows(key, part):
    rows_out = rough_rows(jax.random.fold_in(key, 31), (TOKENS, KVH * HD))
    return rows_out.astype(jnp.bfloat16)


def draw_query_rows(key, part):
    rows_out = rough_rows(jax.random.fold_in(key, 37), (TOKENS, QH * HD))
    return rows_out.astype(jnp.bfloat16)


def steps_of(stream_key, extent, cuts, low, high):
    def one(axis_at, blocks):
        heights = jax.random.uniform(jax.random.fold_in(jax.random.fold_in(stream_key, 6), axis_at), (blocks,), jnp.float32, low / len(cuts), high / len(cuts))
        return jnp.repeat(jnp.exp(heights), extent[axis_at] // blocks).reshape((-1,) + (1,) * (len(extent) - axis_at - 1))

    loudness = one(*cuts[0])
    for cut in cuts[1:]:
        loudness = loudness * one(*cut)
    return loudness


def gaussian(stream_key, extent, deviation, most, cuts=(), kind=jnp.bfloat16):
    values = jax.random.normal(stream_key, extent, jnp.float32) * deviation
    if len(cuts) > 0:
        values = steps_of(stream_key, extent, cuts, -0.22, 0.18) * values
    return jnp.clip(values, min=-most, max=most).astype(kind)


def setup_inputs(seed: int = 0) -> dict:
    streams_of = jax.random.split(jax.random.key(seed), 6)
    query_rows = draw_query_rows(jax.random.fold_in(streams_of[5], 71), 0)
    key_rows = draw_key_rows(jax.random.fold_in(streams_of[5], 71), 0)
    value_rows = gaussian(streams_of[2], (TOKENS, KVH * HD), 1.0, 6.0, ((0, 32),))
    out_grad = gaussian(streams_of[3], (TOKENS, QH * HD), 1.0, 6.0, ((0, 32),))
    doc_lengths = draw_doc_lengths(jax.random.fold_in(streams_of[5], 71), 0)
    return {"query_rows": query_rows, "key_rows": key_rows, "value_rows": value_rows, "out_grad": out_grad, "doc_lengths": doc_lengths}


def reference(query_rows, key_rows, value_rows, out_grad, doc_lengths):
    per_kv = QH // KVH
    scaling = HD ** -0.5
    doc_ends = jnp.cumsum(doc_lengths).astype(jnp.int32)
    positions = jnp.arange(TOKENS, dtype=jnp.int32)
    segments = jnp.sum((positions[:, None] >= doc_ends[None, :]).astype(jnp.int32), axis=1).astype(jnp.int32)
    keys_wide = key_rows.reshape(TOKENS, KVH, HD).astype(jnp.float32)
    values_wide = value_rows.reshape(TOKENS, KVH, HD).astype(jnp.float32)
    block_rows = math.gcd(TOKENS, 512)
    block_count = TOKENS // block_rows
    window = min(TOKENS, LONG + block_rows)

    def window_start(first_row):
        return jnp.clip(first_row + block_rows - window, 0, TOKENS - window).astype(jnp.int32)

    def visible_block(first_row, key_start):
        query_pos = first_row + jnp.arange(block_rows, dtype=jnp.int32)
        query_seg = lax.dynamic_slice_in_dim(segments, first_row, block_rows, 0)
        key_pos = key_start + jnp.arange(window, dtype=jnp.int32)
        key_seg = lax.dynamic_slice_in_dim(segments, key_start, window, 0)
        visible = (key_pos[None, :] <= query_pos[:, None]) & (key_seg[None, :] == query_seg[:, None])
        return visible[:, None, None, :]

    def query_block_of(first_row):
        picked = lax.dynamic_slice_in_dim(query_rows, first_row, block_rows, 0)
        return picked.reshape(block_rows, KVH, per_kv, HD).astype(jnp.float32)

    def forward_block(block_index):
        first_row = (block_index * block_rows).astype(jnp.int32)
        key_start = window_start(first_row)
        spread = visible_block(first_row, key_start)
        keys_near = lax.dynamic_slice_in_dim(keys_wide, key_start, window, 0)
        values_near = lax.dynamic_slice_in_dim(values_wide, key_start, window, 0)
        scores = jnp.einsum("bkgd,tkd->bkgt", query_block_of(first_row), keys_near) * scaling
        scores = jnp.where(spread, scores, -1e30)
        largest = jnp.max(scores, axis=-1)
        weight = jnp.where(spread, jnp.exp(scores - largest[..., None]), 0.0)
        denominator = jnp.sum(weight, axis=-1)
        rounded = lax.optimization_barrier(weight.astype(jnp.bfloat16)).astype(jnp.float32)
        mixed = jnp.einsum("bkgt,tkd->bkgd", rounded, values_near) / denominator[..., None]
        return mixed.astype(jnp.bfloat16).reshape(block_rows, QH * HD), largest + jnp.log(denominator)

    out_blocks, log_blocks = lax.map(forward_block, jnp.arange(block_count, dtype=jnp.int32))
    attended = out_blocks.reshape(TOKENS, QH * HD)
    log_total = log_blocks.reshape(TOKENS, KVH, per_kv)
    grad_wide = out_grad.reshape(TOKENS, KVH, per_kv, HD).astype(jnp.float32)
    row_dot = jnp.sum(grad_wide * attended.reshape(TOKENS, KVH, per_kv, HD).astype(jnp.float32), axis=-1)

    def backward_block(carried, block_index):
        key_sum, value_sum = carried
        first_row = (block_index * block_rows).astype(jnp.int32)
        key_start = window_start(first_row)
        spread = visible_block(first_row, key_start)
        keys_near = lax.dynamic_slice_in_dim(keys_wide, key_start, window, 0)
        values_near = lax.dynamic_slice_in_dim(values_wide, key_start, window, 0)
        query_block = query_block_of(first_row)
        scores = jnp.einsum("bkgd,tkd->bkgt", query_block, keys_near) * scaling
        scores = jnp.where(spread, scores, -1e30)
        log_block = lax.dynamic_slice_in_dim(log_total, first_row, block_rows, 0)
        row_block = lax.dynamic_slice_in_dim(row_dot, first_row, block_rows, 0)
        grad_block = lax.dynamic_slice_in_dim(grad_wide, first_row, block_rows, 0)
        probability = jnp.where(spread, jnp.exp(scores - log_block[..., None]), 0.0)
        prob_rounded = lax.optimization_barrier(probability.astype(jnp.bfloat16)).astype(jnp.float32)
        value_part = jnp.einsum("bkgt,bkgd->tkd", prob_rounded, grad_block)
        grad_prob = jnp.einsum("bkgd,tkd->bkgt", grad_block, values_near)
        grad_score = probability * (grad_prob - row_block[..., None])
        grad_score = lax.optimization_barrier(grad_score.astype(jnp.bfloat16)).astype(jnp.float32)
        query_part = jnp.einsum("bkgt,tkd->bkgd", grad_score, keys_near) * scaling
        key_part = jnp.einsum("bkgt,bkgd->tkd", grad_score, query_block) * scaling
        key_now = lax.dynamic_slice_in_dim(key_sum, key_start, window, 0)
        value_now = lax.dynamic_slice_in_dim(value_sum, key_start, window, 0)
        key_sum = lax.dynamic_update_slice_in_dim(key_sum, key_now + key_part, key_start, 0)
        value_sum = lax.dynamic_update_slice_in_dim(value_sum, value_now + value_part, key_start, 0)
        return (key_sum, value_sum), query_part.astype(jnp.bfloat16).reshape(block_rows, QH * HD)

    zero_sums = jnp.zeros((TOKENS, KVH, HD), jnp.float32)
    (key_sum, value_sum), query_blocks = lax.scan(backward_block, (zero_sums, zero_sums), jnp.arange(block_count, dtype=jnp.int32))
    query_grad = query_blocks.reshape(TOKENS, QH * HD)
    key_grad = key_sum.astype(jnp.bfloat16).reshape(TOKENS, KVH * HD)
    value_grad = value_sum.astype(jnp.bfloat16).reshape(TOKENS, KVH * HD)
    return (attended, query_grad, key_grad, value_grad)
```

```python
import math

import jax
import jax.numpy as jnp
from jax import lax
from jax.experimental import pallas as pl
from jax.experimental.pallas import tpu as pltpu
from jax.sharding import PartitionSpec as P

HD = 128
QH = 20
KVH = 4
GROUP = QH // KVH
HALF_Q = QH // 2
HALF_KV = KVH // 2
MESH = pl.DeviceIdType.MESH
F32 = jnp.float32
BF16 = jnp.bfloat16


def dot_nt(a, b):
    return lax.dot_general(a, b, (((1,), (1,)), ((), ())), preferred_element_type=F32)


def dot_nn(a, b):
    return lax.dot_general(a, b, (((1,), (0,)), ((), ())), preferred_element_type=F32)


def kernel(
    tp,
    window,
    planes,
    q_ref,
    k_ref,
    v_ref,
    g_ref,
    len_ref,
    o_ref,
    dq_ref,
    dk_ref,
    dv_ref,
    kv,
    qs,
    gs,
    q_stage,
    g_stage,
    kv_stage,
    psave,
    msave,
    m_cur,
    l_cur,
    acc,
    row_dot,
    dq_acc,
    bias,
    part,
    part_in,
    own_part,
    z_out,
    z_in,
    o_all,
    o_in,
    dq_all,
    dq_in,
    f_out,
    f_in,
    ex_send,
    ex_recv,
    z_sems,
    plane_send,
    plane_recv,
    part_send,
    part_recv,
    fin_send,
    fin_recv,
):
    rows = q_ref.shape[0]
    pair_rows = 2 * rows
    wide = HALF_KV * HD
    own = window
    me = lax.axis_index("seq") * tp + lax.axis_index("tp")
    core = me % 2
    pair = me // 2
    plane = pair // window
    spot = pair % window
    has_prev = plane > 0
    has_next = plane < planes - 1
    low = core == 0
    mine = pl.multiple_of(core * rows, rows)
    theirs = pl.multiple_of((1 - core) * rows, rows)

    def device(index):
        return (index // tp, index % tp)

    def chip(in_plane, which_plane):
        return device(2 * (which_plane * window + in_plane) + core)

    partner = device(2 * pair + 1 - core)

    def remote(src, dst, send_sem, recv_sem, target):
        return pltpu.make_async_remote_copy(
            src_ref=src,
            dst_ref=dst,
            send_sem=send_sem,
            recv_sem=recv_sem,
            device_id=target,
            device_id_type=MESH,
        )

    barrier = pltpu.get_barrier_semaphore()
    pl.semaphore_signal(barrier, inc=1, device_id=partner, device_id_type=MESH)
    for delta in range(1, window):
        pl.semaphore_signal(
            barrier,
            inc=1,
            device_id=chip((spot + delta) % window, plane),
            device_id_type=MESH,
        )

    @pl.when(has_prev)
    def _():
        pl.semaphore_signal(
            barrier, inc=1, device_id=chip(spot, plane - 1), device_id_type=MESH
        )

    @pl.when(has_next)
    def _():
        pl.semaphore_signal(
            barrier, inc=1, device_id=chip(spot, plane + 1), device_id_type=MESH
        )

    k_all = k_ref[...]
    v_all = v_ref[...]
    kv_stage[0] = jnp.where(low, k_all[:, wide:], k_all[:, :wide])
    kv_stage[1] = jnp.where(low, v_all[:, wide:], v_all[:, :wide])
    kv[own, 0, pl.ds(mine, rows), :] = jnp.where(low, k_all[:, :wide], k_all[:, wide:])
    kv[own, 1, pl.ds(mine, rows), :] = jnp.where(low, v_all[:, :wide], v_all[:, wide:])
    for stage, held, ref in ((q_stage, qs, q_ref), (g_stage, gs, g_ref)):
        for head in range(HALF_Q):
            left = ref[:, head * HD : (head + 1) * HD]
            right = ref[:, (head + HALF_Q) * HD : (head + HALF_Q + 1) * HD]
            stage[head] = jnp.where(low, right, left)
            held[head, pl.ds(mine, rows), :] = jnp.where(low, left, right)

    neighbours = has_prev.astype(jnp.int32) + has_next.astype(jnp.int32)
    pl.semaphore_wait(barrier, window + neighbours)

    kv_swap = remote(
        kv_stage,
        kv.at[own, :, pl.ds(mine, rows), :],
        ex_send.at[0],
        ex_recv.at[0],
        partner,
    )
    q_swap = remote(
        q_stage, qs.at[:, pl.ds(mine, rows), :], ex_send.at[1], ex_recv.at[1], partner
    )
    g_swap = remote(
        g_stage, gs.at[:, pl.ds(mine, rows), :], ex_send.at[2], ex_recv.at[2], partner
    )
    kv_swap.start()
    q_swap.start()
    kv_swap.wait_recv()

    z_send_copy = remote(
        kv.at[own], kv.at[spot], z_sems.at[0], z_sems.at[1], chip(spot, plane + 1)
    )
    z_recv_copy = remote(
        kv.at[own], kv.at[spot], z_sems.at[0], z_sems.at[1], partner
    )

    @pl.when(has_next)
    def _():
        z_send_copy.start()

    def plane_copy(delta, source):
        return remote(
            source,
            kv.at[spot],
            plane_send.at[delta],
            plane_recv.at[spot],
            chip((spot + delta) % window, plane),
        )

    for delta in range(1, window):

        @pl.when(spot + delta < window)
        def _(delta=delta):
            plane_copy(delta, kv.at[own]).start()

    g_swap.start()

    ends = []
    total = jnp.int32(0)
    for doc in range(len_ref.shape[0]):
        total = total + len_ref[doc]
        ends.append(total)
    query_pos = pair * pair_rows + lax.broadcasted_iota(jnp.int32, (1, pair_rows), 1)
    first_key = jnp.zeros((1, pair_rows), jnp.int32)
    for end in ends:
        first_key = jnp.where(query_pos >= end, end, first_key)

    factor2 = HD ** (-0.5) * math.log2(math.e)
    scaling = HD ** (-0.5)

    def absorb(slot, block, first):
        key_pos = block * pair_rows + lax.broadcasted_iota(
            jnp.int32, (pair_rows, pair_rows), 0
        )
        bias[...] = jnp.where(
            (key_pos <= query_pos) & (key_pos >= first_key), 0.0, -1e30
        )
        for kv_head in range(HALF_KV):
            columns = slice(kv_head * HD, (kv_head + 1) * HD)
            key_block = kv[slot, 0, :, columns]
            value_turned = kv[slot, 1, :, columns].T
            for within in range(GROUP):
                head = kv_head * GROUP + within
                score = dot_nt(key_block, qs[head]) * factor2 + bias[...]
                newest = jnp.max(score, axis=0, keepdims=True)
                if not first:
                    newest = jnp.maximum(m_cur[head], newest)
                weight = jnp.exp2(score - newest)
                row_sum = jnp.sum(weight, axis=0, keepdims=True)
                weight_bf = weight.astype(BF16)
                psave[slot, head] = weight_bf
                msave[slot, head] = newest
                product = dot_nn(value_turned, weight_bf)
                if first:
                    l_cur[head] = row_sum
                    acc[head] = product
                else:
                    shrink = jnp.exp2(m_cur[head] - newest)
                    l_cur[head] = l_cur[head] * shrink + row_sum
                    acc[head] = acc[head] * shrink + product
                m_cur[head] = newest

    q_swap.wait_recv()
    absorb(own, pair, True)

    @pl.when(has_prev)
    def _():
        z_recv_copy.wait_recv()
        for delta in range(1, window):

            @pl.when(spot + delta >= window)
            def _(delta=delta):
                plane_copy(delta, kv.at[spot]).start()

    def forward_step(turn, carried):
        slot = jnp.where(turn < spot, spot - 1 - turn, turn)

        @pl.when((slot < spot) | has_prev)
        def _():
            @pl.when(slot != spot)
            def _():
                remote(
                    kv.at[own],
                    kv.at[slot],
                    plane_send.at[0],
                    plane_recv.at[slot],
                    partner,
                ).wait_recv()

            block = jnp.where(slot < spot, plane, plane - 1) * window + slot
            absorb(slot, block, False)

        return carried

    lax.fori_loop(0, window, forward_step, 0)
    g_swap.wait_recv()

    for head in range(HALF_Q):
        inverse = 1.0 / l_cur[head]
        out_turned = acc[head] * inverse
        o_all[head] = out_turned.T.astype(BF16)
        grad_turned = gs[head].astype(F32).T
        row_dot[head] = jnp.sum(
            grad_turned * out_turned.astype(BF16).astype(F32), axis=0, keepdims=True
        )
        l_cur[head] = inverse
        dq_acc[head] = jnp.zeros((HD, pair_rows), F32)

    o_swap = remote(
        o_all.at[:, pl.ds(theirs, rows), :], o_in, fin_send.at[0], fin_recv.at[0], partner
    )
    o_swap.start()

    def contribute(slot, put):
        for kv_head in range(HALF_KV):
            columns = slice(kv_head * HD, (kv_head + 1) * HD)
            key_turned = kv[slot, 0, :, columns].T
            value_block = kv[slot, 1, :, columns]
            key_sum = jnp.zeros((pair_rows, HD), F32)
            value_sum = jnp.zeros((pair_rows, HD), F32)
            for within in range(GROUP):
                head = kv_head * GROUP + within
                level = jnp.exp2(msave[slot, head] - m_cur[head]) * l_cur[head]
                probability = psave[slot, head].astype(F32) * level
                grad_prob = dot_nt(value_block, gs[head])
                grad_score = (probability * (grad_prob - row_dot[head])).astype(BF16)
                value_sum = value_sum + dot_nn(probability.astype(BF16), gs[head])
                key_sum = key_sum + dot_nn(grad_score, qs[head])
                dq_acc[head] = dq_acc[head] + dot_nn(key_turned, grad_score)
            put(0, columns, key_sum * scaling)
            put(1, columns, value_sum)

    def part_copy(slot):
        return remote(
            part.at[slot],
            part_in.at[spot],
            part_send.at[slot],
            part_recv.at[spot],
            chip(slot, plane),
        )

    def backward_step(turn, carried):
        slot = window - 1 - turn

        @pl.when((slot < spot) | has_prev)
        def _():
            def put(which, columns, value):
                part[slot, which, :, columns] = value.astype(BF16)

            contribute(slot, put)

            @pl.when(slot != spot)
            def _():
                part_copy(slot).start()

        return carried

    lax.fori_loop(0, window, backward_step, 0)

    def part_arrived(slot):
        remote(
            part.at[slot], part_in.at[slot], part_send.at[slot], part_recv.at[slot], partner
        ).wait_recv()

    z_back = remote(z_out, z_in, z_sems.at[2], z_sems.at[3], chip(spot, plane - 1))
    z_back_in = remote(z_out, z_in, z_sems.at[2], z_sems.at[3], partner)

    @pl.when(has_prev)
    def _():
        own_part[...] = part[spot].astype(F32)

        def gather(slot, carried):
            part_arrived(slot)
            own_part[...] += part_in[slot].astype(F32)
            return carried

        lax.fori_loop(0, spot, gather, 0)
        z_out[...] = own_part[...].astype(BF16)
        z_back.start()

    def put_own(which, columns, value):
        own_part[which, :, columns] = value

    contribute(own, put_own)

    for head in range(HALF_Q):
        dq_all[head] = (dq_acc[head] * scaling).T.astype(BF16)
    dq_swap = remote(
        dq_all.at[:, pl.ds(theirs, rows), :],
        dq_in,
        fin_send.at[1],
        fin_recv.at[1],
        partner,
    )
    dq_swap.start()

    def gather_own(slot, carried):
        part_arrived(slot)
        own_part[...] += part_in[slot].astype(F32)
        return carried

    lax.fori_loop(spot + 1, window, gather_own, 0)

    o_swap.wait_recv()
    dq_swap.wait_recv()
    for ref, everything, arrived in ((o_ref, o_all, o_in), (dq_ref, dq_all, dq_in)):
        for head in range(HALF_Q):
            here = everything[head, pl.ds(mine, rows), :]
            there = arrived[head]
            ref[:, head * HD : (head + 1) * HD] = jnp.where(low, here, there)
            ref[:, (head + HALF_Q) * HD : (head + HALF_Q + 1) * HD] = jnp.where(
                low, there, here
            )

    @pl.when(has_next)
    def _():
        z_back_in.wait_recv()
        own_part[...] += z_in[...].astype(F32)

    f_out[...] = own_part[:, pl.ds(theirs, rows), :].astype(BF16)
    f_swap = remote(f_out, f_in, fin_send.at[2], fin_recv.at[2], partner)
    f_swap.start()
    f_swap.wait_recv()
    for which, ref in ((0, dk_ref), (1, dv_ref)):
        here = own_part[which, pl.ds(mine, rows), :].astype(BF16)
        there = f_in[which]
        ref[:, :wide] = jnp.where(low, here, there)
        ref[:, wide:] = jnp.where(low, there, here)

    for copy in (kv_swap, q_swap, g_swap, o_swap, dq_swap, f_swap):
        copy.wait_send()

    @pl.when(has_next)
    def _():
        z_send_copy.wait_send()

    @pl.when(has_prev)
    def _():
        z_back.wait_send()

    for delta in range(1, window):

        @pl.when((spot + delta < window) | has_prev)
        def _(delta=delta):
            plane_copy(delta, kv.at[own]).wait_send()

    def sent(slot, carried):
        @pl.when(((slot < spot) | has_prev) & (slot != spot))
        def _():
            part_copy(slot).wait_send()

        return carried

    lax.fori_loop(0, window, sent, 0)


def per_device(seq, tp, query_rows, key_rows, value_rows, out_grad, doc_lengths):
    rows = query_rows.shape[0]
    pairs = seq * tp // 2
    planes = 4
    window = pairs // planes
    pair_rows = 2 * rows
    wide = HALF_KV * HD
    blocks = window + 1
    dma = pltpu.SemaphoreType.DMA
    vmem = pltpu.VMEM
    scratch = [
        vmem((blocks, 2, pair_rows, wide), BF16),
        vmem((HALF_Q, pair_rows, HD), BF16),
        vmem((HALF_Q, pair_rows, HD), BF16),
        vmem((HALF_Q, rows, HD), BF16),
        vmem((HALF_Q, rows, HD), BF16),
        vmem((2, rows, wide), BF16),
        vmem((blocks, HALF_Q, pair_rows, pair_rows), BF16),
        vmem((blocks, HALF_Q, 1, pair_rows), F32),
        vmem((HALF_Q, 1, pair_rows), F32),
        vmem((HALF_Q, 1, pair_rows), F32),
        vmem((HALF_Q, HD, pair_rows), F32),
        vmem((HALF_Q, 1, pair_rows), F32),
        vmem((HALF_Q, HD, pair_rows), F32),
        vmem((pair_rows, pair_rows), F32),
        vmem((window, 2, pair_rows, wide), BF16),
        vmem((window, 2, pair_rows, wide), BF16),
        vmem((2, pair_rows, wide), F32),
        vmem((2, pair_rows, wide), BF16),
        vmem((2, pair_rows, wide), BF16),
        vmem((HALF_Q, pair_rows, HD), BF16),
        vmem((HALF_Q, rows, HD), BF16),
        vmem((HALF_Q, pair_rows, HD), BF16),
        vmem((HALF_Q, rows, HD), BF16),
        vmem((2, rows, wide), BF16),
        vmem((2, rows, wide), BF16),
        dma((3,)),
        dma((3,)),
        dma((4,)),
        dma((window,)),
        dma((window,)),
        dma((window,)),
        dma((window,)),
        dma((3,)),
        dma((3,)),
    ]
    whole = pl.BlockSpec(memory_space=pltpu.VMEM)

    def body(*refs):
        kernel(tp, window, planes, *refs)

    return pl.pallas_call(
        body,
        out_shape=tuple(
            jax.ShapeDtypeStruct(x.shape, BF16)
            for x in (query_rows, query_rows, key_rows, value_rows)
        ),
        in_specs=[whole] * 4 + [pl.BlockSpec(memory_space=pltpu.SMEM)],
        out_specs=(whole,) * 4,
        scratch_shapes=scratch,
        compiler_params=pltpu.CompilerParams(
            collective_id=0,
            has_side_effects=True,
            vmem_limit_bytes=60 * 2**20,
        ),
        name="packed_attention",
    )(query_rows, key_rows, value_rows, out_grad, doc_lengths)


def solution(mesh):
    seq, tp = mesh.shape["seq"], mesh.shape["tp"]
    spec = P(("seq", "tp"), None)

    def run(*args):
        return per_device(seq, tp, *args)

    return jax.shard_map(
        run,
        mesh=mesh,
        in_specs=(spec, spec, spec, spec, P()),
        out_specs=(spec,) * 4,
        check_vma=False,
    )
```

```python
import math

import jax
import jax.numpy as jnp
from jax import lax
from jax.experimental import pallas as pl
from jax.experimental.pallas import tpu as pltpu
from jax.sharding import PartitionSpec as P

HD = 128
QH = 20
KVH = 4
GROUP = QH // KVH
HALF_Q = QH // 2
HALF_KV = KVH // 2
CHUNK = 128
MESH = pl.DeviceIdType.MESH
F32 = jnp.float32
BF16 = jnp.bfloat16


def dot_nt(a, b):
    return lax.dot_general(a, b, (((1,), (1,)), ((), ())), preferred_element_type=F32)


def dot_nn(a, b):
    return lax.dot_general(a, b, (((1,), (0,)), ((), ())), preferred_element_type=F32)


def kernel(
    tp,
    window,
    planes,
    q_ref,
    k_ref,
    v_ref,
    g_ref,
    len_ref,
    o_ref,
    dq_ref,
    dk_ref,
    dv_ref,
    kv,
    qs,
    gs,
    q_stage,
    g_stage,
    kv_stage,
    psave,
    msave,
    m_cur,
    l_cur,
    shrinks,
    acc,
    row_dot,
    dq_acc,
    bias,
    q_turned,
    g_turned,
    wide_buf,
    p_buf,
    ds_buf,
    part,
    part_in,
    own_part,
    z_out,
    z_in,
    o_all,
    o_in,
    dq_all,
    dq_in,
    f_out,
    f_in,
    ex_send,
    ex_recv,
    z_sems,
    plane_send,
    plane_recv,
    part_send,
    part_recv,
    fin_send,
    fin_recv,
):
    rows = q_ref.shape[0]
    pair_rows = 2 * rows
    wide = HALF_KV * HD
    own = window
    me = lax.axis_index("seq") * tp + lax.axis_index("tp")
    core = me % 2
    pair = me // 2
    plane = pair // window
    spot = pair % window
    has_prev = plane > 0
    has_next = plane < planes - 1
    low = core == 0
    mine = pl.multiple_of(core * rows, rows)
    theirs = pl.multiple_of((1 - core) * rows, rows)

    def device(index):
        return (index // tp, index % tp)

    def chip(in_plane, which_plane):
        return device(2 * (which_plane * window + in_plane) + core)

    partner = device(2 * pair + 1 - core)

    def head_lanes(head):
        kv_head, within = divmod(head, GROUP)
        return kv_head, slice(within * pair_rows, (within + 1) * pair_rows)

    def remote(src, dst, send_sem, recv_sem, target):
        return pltpu.make_async_remote_copy(
            src_ref=src,
            dst_ref=dst,
            send_sem=send_sem,
            recv_sem=recv_sem,
            device_id=target,
            device_id_type=MESH,
        )

    barrier = pltpu.get_barrier_semaphore()
    pl.semaphore_signal(barrier, inc=1, device_id=partner, device_id_type=MESH)
    for delta in range(1, window):
        pl.semaphore_signal(
            barrier,
            inc=1,
            device_id=chip((spot + delta) % window, plane),
            device_id_type=MESH,
        )

    @pl.when(has_prev)
    def _():
        pl.semaphore_signal(
            barrier, inc=1, device_id=chip(spot, plane - 1), device_id_type=MESH
        )

    @pl.when(has_next)
    def _():
        pl.semaphore_signal(
            barrier, inc=1, device_id=chip(spot, plane + 1), device_id_type=MESH
        )

    k_all = k_ref[...]
    v_all = v_ref[...]
    kv_stage[0] = jnp.where(low, k_all[:, wide:], k_all[:, :wide])
    kv_stage[1] = jnp.where(low, v_all[:, wide:], v_all[:, :wide])
    kv[own, 0, pl.ds(mine, rows), :] = jnp.where(low, k_all[:, :wide], k_all[:, wide:])
    kv[own, 1, pl.ds(mine, rows), :] = jnp.where(low, v_all[:, :wide], v_all[:, wide:])
    for stage, held, ref in ((q_stage, qs, q_ref), (g_stage, gs, g_ref)):
        for head in range(HALF_Q):
            left = ref[:, head * HD : (head + 1) * HD]
            right = ref[:, (head + HALF_Q) * HD : (head + HALF_Q + 1) * HD]
            stage[head] = jnp.where(low, right, left)
            held[head, pl.ds(mine, rows), :] = jnp.where(low, left, right)

    neighbours = has_prev.astype(jnp.int32) + has_next.astype(jnp.int32)
    pl.semaphore_wait(barrier, window + neighbours)

    kv_swap = remote(
        kv_stage,
        kv.at[own, :, pl.ds(mine, rows), :],
        ex_send.at[0],
        ex_recv.at[0],
        partner,
    )
    q_swap = remote(
        q_stage, qs.at[:, pl.ds(mine, rows), :], ex_send.at[1], ex_recv.at[1], partner
    )
    g_swap = remote(
        g_stage, gs.at[:, pl.ds(mine, rows), :], ex_send.at[2], ex_recv.at[2], partner
    )
    kv_swap.start()
    q_swap.start()
    kv_swap.wait_recv()

    z_send_copy = remote(
        kv.at[own], kv.at[spot], z_sems.at[0], z_sems.at[1], chip(spot, plane + 1)
    )
    z_recv_copy = remote(
        kv.at[own], kv.at[spot], z_sems.at[0], z_sems.at[1], partner
    )

    @pl.when(has_next)
    def _():
        z_send_copy.start()

    def plane_copy(delta, source):
        return remote(
            source,
            kv.at[spot],
            plane_send.at[delta],
            plane_recv.at[spot],
            chip((spot + delta) % window, plane),
        )

    for delta in range(1, window):

        @pl.when(spot + delta < window)
        def _(delta=delta):
            plane_copy(delta, kv.at[own]).start()

    g_swap.start()

    ends = []
    total = jnp.int32(0)
    for doc in range(len_ref.shape[0]):
        total = total + len_ref[doc]
        ends.append(total)
    query_pos = pair * pair_rows + lax.broadcasted_iota(jnp.int32, (1, pair_rows), 1)
    first_key = jnp.zeros((1, pair_rows), jnp.int32)
    for end in ends:
        first_key = jnp.where(query_pos >= end, end, first_key)

    factor2 = HD ** (-0.5) * math.log2(math.e)
    scaling = HD ** (-0.5)

    def absorb(slot, block, first):
        key_pos = block * pair_rows + lax.broadcasted_iota(
            jnp.int32, (pair_rows, pair_rows), 0
        )
        bias[...] = jnp.where(
            (key_pos <= query_pos) & (key_pos >= first_key), 0.0, -1e30
        )
        for kv_head in range(HALF_KV):
            columns = slice(kv_head * HD, (kv_head + 1) * HD)
            wide_buf[kv_head] = dot_nn(kv[slot, 0, :, columns], q_turned[kv_head])
        for kv_head in range(HALF_KV):
            columns = slice(kv_head * HD, (kv_head + 1) * HD)
            for at in range(0, GROUP * pair_rows, CHUNK):
                lanes = slice(at, at + CHUNK)
                tokens = slice(at % pair_rows, at % pair_rows + CHUNK)
                score = wide_buf[kv_head, :, lanes] * factor2 + bias[:, tokens]
                newest = jnp.max(score, axis=0, keepdims=True)
                if not first:
                    before = m_cur[kv_head, :, lanes]
                    newest = jnp.maximum(before, newest)
                weight = jnp.exp2(score - newest)
                row_sum = jnp.sum(weight, axis=0, keepdims=True)
                psave[slot, kv_head, :, lanes] = weight.astype(BF16)
                msave[slot, kv_head, :, lanes] = newest
                if not first:
                    shrink = jnp.exp2(before - newest)
                    row_sum = l_cur[kv_head, :, lanes] * shrink + row_sum
                    shrinks[kv_head, :, lanes] = shrink
                l_cur[kv_head, :, lanes] = row_sum
                m_cur[kv_head, :, lanes] = newest
            product = dot_nn(kv[slot, 1, :, columns].T, psave[slot, kv_head])
            if first:
                acc[kv_head] = product
            else:
                acc[kv_head] = acc[kv_head] * shrinks[kv_head] + product

    q_swap.wait_recv()
    for head in range(HALF_Q):
        kv_head, lanes = head_lanes(head)
        q_turned[kv_head, :, lanes] = qs[head].T
    absorb(own, pair, True)

    @pl.when(has_prev)
    def _():
        z_recv_copy.wait_recv()
        for delta in range(1, window):

            @pl.when(spot + delta >= window)
            def _(delta=delta):
                plane_copy(delta, kv.at[spot]).start()

    def forward_step(turn, carried):
        slot = jnp.where(turn < spot, spot - 1 - turn, turn)

        @pl.when((slot < spot) | has_prev)
        def _():
            @pl.when(slot != spot)
            def _():
                remote(
                    kv.at[own],
                    kv.at[slot],
                    plane_send.at[0],
                    plane_recv.at[slot],
                    partner,
                ).wait_recv()

            block = jnp.where(slot < spot, plane, plane - 1) * window + slot
            absorb(slot, block, False)

        return carried

    lax.fori_loop(0, window, forward_step, 0)
    g_swap.wait_recv()

    for head in range(HALF_Q):
        kv_head, lanes = head_lanes(head)
        inverse = 1.0 / l_cur[kv_head, :, lanes]
        out_turned = acc[kv_head, :, lanes] * inverse
        o_all[head] = out_turned.T.astype(BF16)
        grad_turned = gs[head].T
        g_turned[kv_head, :, lanes] = grad_turned
        row_dot[kv_head, :, lanes] = jnp.sum(
            grad_turned.astype(F32) * out_turned.astype(BF16).astype(F32),
            axis=0,
            keepdims=True,
        )
        l_cur[kv_head, :, lanes] = inverse
    dq_acc[...] = jnp.zeros_like(dq_acc)

    o_swap = remote(
        o_all.at[:, pl.ds(theirs, rows), :], o_in, fin_send.at[0], fin_recv.at[0], partner
    )
    o_swap.start()

    def contribute(slot, put):
        for kv_head in range(HALF_KV):
            columns = slice(kv_head * HD, (kv_head + 1) * HD)
            wide_buf[kv_head] = dot_nn(kv[slot, 1, :, columns], g_turned[kv_head])
        for kv_head in range(HALF_KV):
            columns = slice(kv_head * HD, (kv_head + 1) * HD)
            heads = slice(kv_head * GROUP, (kv_head + 1) * GROUP)
            stacked = (GROUP * pair_rows, HD)
            for at in range(0, GROUP * pair_rows, CHUNK):
                lanes = slice(at, at + CHUNK)
                level = (
                    jnp.exp2(msave[slot, kv_head, :, lanes] - m_cur[kv_head, :, lanes])
                    * l_cur[kv_head, :, lanes]
                )
                probability = psave[slot, kv_head, :, lanes].astype(F32) * level
                grad_prob = wide_buf[kv_head, :, lanes]
                grad_score = probability * (grad_prob - row_dot[kv_head, :, lanes])
                p_buf[kv_head, :, lanes] = probability.astype(BF16)
                ds_buf[kv_head, :, lanes] = grad_score.astype(BF16)
            put(1, columns, dot_nn(p_buf[kv_head], gs[heads].reshape(stacked)))
            put(
                0,
                columns,
                dot_nn(ds_buf[kv_head], qs[heads].reshape(stacked)) * scaling,
            )
            dq_acc[kv_head] = dq_acc[kv_head] + dot_nn(
                kv[slot, 0, :, columns].T, ds_buf[kv_head]
            )

    def part_copy(slot):
        return remote(
            part.at[slot],
            part_in.at[spot],
            part_send.at[slot],
            part_recv.at[spot],
            chip(slot, plane),
        )

    def backward_step(turn, carried):
        slot = window - 1 - turn

        @pl.when((slot < spot) | has_prev)
        def _():
            def put(which, columns, value):
                part[slot, which, :, columns] = value.astype(BF16)

            contribute(slot, put)

            @pl.when(slot != spot)
            def _():
                part_copy(slot).start()

        return carried

    lax.fori_loop(0, window, backward_step, 0)

    def part_arrived(slot):
        remote(
            part.at[slot], part_in.at[slot], part_send.at[slot], part_recv.at[slot], partner
        ).wait_recv()

    z_back = remote(z_out, z_in, z_sems.at[2], z_sems.at[3], chip(spot, plane - 1))
    z_back_in = remote(z_out, z_in, z_sems.at[2], z_sems.at[3], partner)

    @pl.when(has_prev)
    def _():
        own_part[...] = part[spot].astype(F32)

        def gather(slot, carried):
            part_arrived(slot)
            own_part[...] += part_in[slot].astype(F32)
            return carried

        lax.fori_loop(0, spot, gather, 0)
        z_out[...] = own_part[...].astype(BF16)
        z_back.start()

    def put_own(which, columns, value):
        own_part[which, :, columns] = value

    contribute(own, put_own)

    for head in range(HALF_Q):
        kv_head, lanes = head_lanes(head)
        dq_all[head] = (dq_acc[kv_head, :, lanes] * scaling).T.astype(BF16)
    dq_swap = remote(
        dq_all.at[:, pl.ds(theirs, rows), :],
        dq_in,
        fin_send.at[1],
        fin_recv.at[1],
        partner,
    )
    dq_swap.start()

    def gather_own(slot, carried):
        part_arrived(slot)
        own_part[...] += part_in[slot].astype(F32)
        return carried

    lax.fori_loop(spot + 1, window, gather_own, 0)

    o_swap.wait_recv()
    dq_swap.wait_recv()
    for ref, everything, arrived in ((o_ref, o_all, o_in), (dq_ref, dq_all, dq_in)):
        for head in range(HALF_Q):
            here = everything[head, pl.ds(mine, rows), :]
            there = arrived[head]
            ref[:, head * HD : (head + 1) * HD] = jnp.where(low, here, there)
            ref[:, (head + HALF_Q) * HD : (head + HALF_Q + 1) * HD] = jnp.where(
                low, there, here
            )

    @pl.when(has_next)
    def _():
        z_back_in.wait_recv()
        own_part[...] += z_in[...].astype(F32)

    f_out[...] = own_part[:, pl.ds(theirs, rows), :].astype(BF16)
    f_swap = remote(f_out, f_in, fin_send.at[2], fin_recv.at[2], partner)
    f_swap.start()
    f_swap.wait_recv()
    for which, ref in ((0, dk_ref), (1, dv_ref)):
        here = own_part[which, pl.ds(mine, rows), :].astype(BF16)
        there = f_in[which]
        ref[:, :wide] = jnp.where(low, here, there)
        ref[:, wide:] = jnp.where(low, there, here)

    for copy in (kv_swap, q_swap, g_swap, o_swap, dq_swap, f_swap):
        copy.wait_send()

    @pl.when(has_next)
    def _():
        z_send_copy.wait_send()

    @pl.when(has_prev)
    def _():
        z_back.wait_send()

    for delta in range(1, window):

        @pl.when((spot + delta < window) | has_prev)
        def _(delta=delta):
            plane_copy(delta, kv.at[own]).wait_send()

    def sent(slot, carried):
        @pl.when(((slot < spot) | has_prev) & (slot != spot))
        def _():
            part_copy(slot).wait_send()

        return carried

    lax.fori_loop(0, window, sent, 0)


def hand_over(*refs):
    for source, target in zip(refs[:4], refs[4:]):
        target[...] = source[...]


def per_device(seq, tp, query_rows, key_rows, value_rows, out_grad, doc_lengths):
    rows = query_rows.shape[0]
    pairs = seq * tp // 2
    planes = 4
    window = pairs // planes
    pair_rows = 2 * rows
    wide = HALF_KV * HD
    blocks = window + 1
    long = GROUP * pair_rows
    dma = pltpu.SemaphoreType.DMA
    vmem = pltpu.VMEM
    scratch = [
        vmem((blocks, 2, pair_rows, wide), BF16),
        vmem((HALF_Q, pair_rows, HD), BF16),
        vmem((HALF_Q, pair_rows, HD), BF16),
        vmem((HALF_Q, rows, HD), BF16),
        vmem((HALF_Q, rows, HD), BF16),
        vmem((2, rows, wide), BF16),
        vmem((blocks, HALF_KV, pair_rows, long), BF16),
        vmem((blocks, HALF_KV, 1, long), F32),
        vmem((HALF_KV, 1, long), F32),
        vmem((HALF_KV, 1, long), F32),
        vmem((HALF_KV, 1, long), F32),
        vmem((HALF_KV, HD, long), F32),
        vmem((HALF_KV, 1, long), F32),
        vmem((HALF_KV, HD, long), F32),
        vmem((pair_rows, pair_rows), F32),
        vmem((HALF_KV, HD, long), BF16),
        vmem((HALF_KV, HD, long), BF16),
        vmem((HALF_KV, pair_rows, long), F32),
        vmem((HALF_KV, pair_rows, long), BF16),
        vmem((HALF_KV, pair_rows, long), BF16),
        vmem((window, 2, pair_rows, wide), BF16),
        vmem((window, 2, pair_rows, wide), BF16),
        vmem((2, pair_rows, wide), F32),
        vmem((2, pair_rows, wide), BF16),
        vmem((2, pair_rows, wide), BF16),
        vmem((HALF_Q, pair_rows, HD), BF16),
        vmem((HALF_Q, rows, HD), BF16),
        vmem((HALF_Q, pair_rows, HD), BF16),
        vmem((HALF_Q, rows, HD), BF16),
        vmem((2, rows, wide), BF16),
        vmem((2, rows, wide), BF16),
        dma((3,)),
        dma((3,)),
        dma((4,)),
        dma((window,)),
        dma((window,)),
        dma((window,)),
        dma((window,)),
        dma((3,)),
        dma((3,)),
    ]
    whole = pl.BlockSpec(memory_space=pltpu.VMEM)

    def body(*refs):
        kernel(tp, window, planes, *refs)

    shapes = tuple(
        jax.ShapeDtypeStruct(x.shape, BF16)
        for x in (query_rows, query_rows, key_rows, value_rows)
    )
    results = pl.pallas_call(
        body,
        out_shape=shapes,
        in_specs=[whole] * 4 + [pl.BlockSpec(memory_space=pltpu.SMEM)],
        out_specs=(whole,) * 4,
        scratch_shapes=scratch,
        compiler_params=pltpu.CompilerParams(
            collective_id=0,
            has_side_effects=True,
            vmem_limit_bytes=60 * 2**20,
        ),
        name="packed_attention",
    )(query_rows, key_rows, value_rows, out_grad, doc_lengths)
    return pl.pallas_call(
        hand_over,
        out_shape=shapes,
        in_specs=[whole] * 4,
        out_specs=(whole,) * 4,
        name="hand_over",
    )(*results)


def solution(mesh):
    seq, tp = mesh.shape["seq"], mesh.shape["tp"]
    spec = P(("seq", "tp"), None)

    def run(*args):
        return per_device(seq, tp, *args)

    return jax.shard_map(
        run,
        mesh=mesh,
        in_specs=(spec, spec, spec, spec, P()),
        out_specs=(spec,) * 4,
        check_vma=False,
    )
```

```python
import math

import jax
import jax.numpy as jnp
from jax import lax
from jax.experimental import pallas as pl
from jax.experimental.pallas import tpu as pltpu
from jax.sharding import PartitionSpec as P

HD = 128
QH = 20
KVH = 4
GROUP = QH // KVH
HALF_Q = QH // 2
HALF_KV = KVH // 2
CHUNK = 128
MESH = pl.DeviceIdType.MESH
F32 = jnp.float32
BF16 = jnp.bfloat16


def dot_nt(a, b):
    return lax.dot_general(a, b, (((1,), (1,)), ((), ())), preferred_element_type=F32)


def dot_nn(a, b):
    return lax.dot_general(a, b, (((1,), (0,)), ((), ())), preferred_element_type=F32)


def kernel(
    tp,
    window,
    planes,
    q_ref,
    k_ref,
    v_ref,
    g_ref,
    len_ref,
    o_ref,
    dq_ref,
    dk_ref,
    dv_ref,
    kv,
    qs,
    gs,
    q_stage,
    g_stage,
    kv_stage,
    psave,
    msave,
    m_cur,
    l_cur,
    shrinks,
    acc,
    row_dot,
    dq_acc,
    bias,
    q_turned,
    g_turned,
    wide_buf,
    p_buf,
    ds_buf,
    part,
    part_in,
    own_part,
    totals,
    z_out,
    z_in,
    o_all,
    o_in,
    dq_all,
    dq_in,
    f_out,
    f_in,
    ex_send,
    ex_recv,
    z_send,
    z_recv,
    z_back_sems,
    plane_send,
    plane_recv,
    part_send,
    part_recv,
    fin_send,
    fin_recv,
):
    rows = q_ref.shape[0]
    pair_rows = 2 * rows
    wide = HALF_KV * HD
    own = window
    me = lax.axis_index("seq") * tp + lax.axis_index("tp")
    core = me % 2
    pair = me // 2
    plane = pair // window
    spot = pair % window
    has_prev = plane > 0
    has_next = plane < planes - 1
    low = core == 0
    mine = pl.multiple_of(core * rows, rows)
    theirs = pl.multiple_of((1 - core) * rows, rows)

    def device(index):
        return (index // tp, index % tp)

    def at_chip(in_plane, which_plane, which_core):
        return device(2 * (which_plane * window + in_plane) + which_core)

    partner = device(2 * pair + 1 - core)

    def head_lanes(head):
        kv_head, within = divmod(head, GROUP)
        return kv_head, slice(within * pair_rows, (within + 1) * pair_rows)

    def remote(src, dst, send_sem, recv_sem, target):
        return pltpu.make_async_remote_copy(
            src_ref=src,
            dst_ref=dst,
            send_sem=send_sem,
            recv_sem=recv_sem,
            device_id=target,
            device_id_type=MESH,
        )

    barrier = pltpu.get_barrier_semaphore()

    def greet(target):
        pl.semaphore_signal(barrier, inc=1, device_id=target, device_id_type=MESH)

    greet(partner)
    for which in range(2):
        for delta in range(1, window):
            greet(at_chip((spot + delta) % window, plane, which))

        @pl.when(has_prev)
        def _(which=which):
            greet(at_chip(spot, plane - 1, which))

        @pl.when(has_next)
        def _(which=which):
            greet(at_chip(spot, plane + 1, which))

    k_all = k_ref[...]
    v_all = v_ref[...]
    for which in range(2):
        half = slice(which * wide, (which + 1) * wide)
        kv_stage[which, 0] = k_all[:, half]
        kv_stage[which, 1] = v_all[:, half]
    kv[own, 0, pl.ds(mine, rows), :] = jnp.where(low, k_all[:, :wide], k_all[:, wide:])
    kv[own, 1, pl.ds(mine, rows), :] = jnp.where(low, v_all[:, :wide], v_all[:, wide:])

    neighbours = has_prev.astype(jnp.int32) + has_next.astype(jnp.int32)
    pl.semaphore_wait(barrier, 2 * window - 1 + 2 * neighbours)

    def z_copy(which, part_of):
        return remote(
            kv_stage.at[which, part_of],
            kv.at[spot, part_of, pl.ds(mine, rows), :],
            z_send.at[which, part_of],
            z_recv.at[core, part_of],
            at_chip(spot, plane + 1, which),
        )

    def z_arrival(row_core, part_of):
        return remote(
            kv_stage.at[0, part_of],
            kv.at[spot, part_of, pl.ds(row_core * rows, rows), :],
            z_send.at[0, part_of],
            z_recv.at[row_core, part_of],
            partner,
        )

    def plane_copy(delta, which):
        return remote(
            kv_stage.at[which],
            kv.at[spot, :, pl.ds(mine, rows), :],
            plane_send.at[delta, which],
            plane_recv.at[spot, core],
            at_chip((spot + delta) % window, plane, which),
        )

    def plane_pass(delta, part_of):
        return remote(
            kv.at[spot, part_of],
            kv.at[spot, part_of],
            plane_send.at[delta, part_of],
            plane_recv.at[spot, part_of],
            at_chip((spot + delta) % window, plane, core),
        )

    kv_swap = remote(
        kv_stage.at[1 - core],
        kv.at[own, :, pl.ds(mine, rows), :],
        ex_send.at[0],
        ex_recv.at[0],
        partner,
    )
    kv_swap.start()

    @pl.when(has_next)
    def _():
        for part_of in range(2):
            for which in range(2):
                z_copy(which, part_of).start()

    for delta in range(1, window):

        @pl.when(spot + delta < window)
        def _(delta=delta):
            for which in range(2):
                plane_copy(delta, which).start()

    swaps = []
    for index, (stage, held, ref) in enumerate(
        ((q_stage, qs, q_ref), (g_stage, gs, g_ref))
    ):
        for head in range(HALF_Q):
            left = ref[:, head * HD : (head + 1) * HD]
            right = ref[:, (head + HALF_Q) * HD : (head + HALF_Q + 1) * HD]
            stage[head] = jnp.where(low, right, left)
            held[head, pl.ds(mine, rows), :] = jnp.where(low, left, right)
        swap = remote(
            stage,
            held.at[:, pl.ds(mine, rows), :],
            ex_send.at[index + 1],
            ex_recv.at[index + 1],
            partner,
        )
        swap.start()
        swaps.append(swap)
    q_swap, g_swap = swaps

    ends = []
    total = jnp.int32(0)
    for doc in range(len_ref.shape[0]):
        total = total + len_ref[doc]
        ends.append(total)
    query_pos = pair * pair_rows + lax.broadcasted_iota(jnp.int32, (1, pair_rows), 1)
    first_key = jnp.zeros((1, pair_rows), jnp.int32)
    for end in ends:
        first_key = jnp.where(query_pos >= end, end, first_key)

    factor2 = HD ** (-0.5) * math.log2(math.e)
    scaling = HD ** (-0.5)

    def absorb(slot, block, first):
        key_pos = block * pair_rows + lax.broadcasted_iota(
            jnp.int32, (pair_rows, pair_rows), 0
        )
        bias[...] = jnp.where(
            (key_pos <= query_pos) & (key_pos >= first_key), 0.0, -1e30
        )
        for kv_head in range(HALF_KV):
            columns = slice(kv_head * HD, (kv_head + 1) * HD)
            wide_buf[kv_head] = dot_nn(kv[slot, 0, :, columns], q_turned[kv_head])
        for kv_head in range(HALF_KV):
            columns = slice(kv_head * HD, (kv_head + 1) * HD)
            for at in range(0, GROUP * pair_rows, CHUNK):
                lanes = slice(at, at + CHUNK)
                tokens = slice(at % pair_rows, at % pair_rows + CHUNK)
                score = wide_buf[kv_head, :, lanes] * factor2 + bias[:, tokens]
                newest = jnp.max(score, axis=0, keepdims=True)
                if not first:
                    before = m_cur[kv_head, :, lanes]
                    newest = jnp.maximum(before, newest)
                weight = jnp.exp2(score - newest)
                row_sum = jnp.sum(weight, axis=0, keepdims=True)
                psave[slot, kv_head, :, lanes] = weight.astype(BF16)
                msave[slot, kv_head, :, lanes] = newest
                if not first:
                    shrink = jnp.exp2(before - newest)
                    row_sum = l_cur[kv_head, :, lanes] * shrink + row_sum
                    shrinks[kv_head, :, lanes] = shrink
                l_cur[kv_head, :, lanes] = row_sum
                m_cur[kv_head, :, lanes] = newest
            product = dot_nn(kv[slot, 1, :, columns].T, psave[slot, kv_head])
            if first:
                acc[kv_head] = product
            else:
                acc[kv_head] = acc[kv_head] * shrinks[kv_head] + product

    q_swap.wait_recv()
    for head in range(HALF_Q):
        kv_head, lanes = head_lanes(head)
        q_turned[kv_head, :, lanes] = qs[head].T
    kv_swap.wait_recv()
    absorb(own, pair, True)

    @pl.when(has_prev)
    def _():
        for part_of in range(2):
            for row_core in range(2):
                z_arrival(row_core, part_of).wait_recv()
            for delta in range(1, window):

                @pl.when(spot + delta >= window)
                def _(delta=delta, part_of=part_of):
                    plane_pass(delta, part_of).start()

    def forward_step(turn, carried):
        slot = jnp.where(turn < spot, spot - 1 - turn, turn)

        @pl.when((slot < spot) | has_prev)
        def _():
            @pl.when(slot < spot)
            def _():
                for row_core in range(2):
                    remote(
                        kv_stage.at[0],
                        kv.at[slot, :, pl.ds(row_core * rows, rows), :],
                        plane_send.at[0, row_core],
                        plane_recv.at[slot, row_core],
                        partner,
                    ).wait_recv()

            @pl.when(slot > spot)
            def _():
                for part_of in range(2):
                    remote(
                        kv.at[own, part_of],
                        kv.at[slot, part_of],
                        plane_send.at[0, part_of],
                        plane_recv.at[slot, part_of],
                        partner,
                    ).wait_recv()

            block = jnp.where(slot < spot, plane, plane - 1) * window + slot
            absorb(slot, block, False)

        return carried

    lax.fori_loop(0, window, forward_step, 0)
    g_swap.wait_recv()

    for head in range(HALF_Q):
        kv_head, lanes = head_lanes(head)
        inverse = 1.0 / l_cur[kv_head, :, lanes]
        out_turned = acc[kv_head, :, lanes] * inverse
        o_all[head] = out_turned.T.astype(BF16)
        grad_turned = gs[head].T
        g_turned[kv_head, :, lanes] = grad_turned
        row_dot[kv_head, :, lanes] = jnp.sum(
            grad_turned.astype(F32) * out_turned.astype(BF16).astype(F32),
            axis=0,
            keepdims=True,
        )
        l_cur[kv_head, :, lanes] = inverse
    dq_acc[...] = jnp.zeros_like(dq_acc)

    o_swap = remote(
        o_all.at[:, pl.ds(theirs, rows), :], o_in, fin_send.at[0], fin_recv.at[0], partner
    )
    o_swap.start()

    def contribute(slot, put):
        for kv_head in range(HALF_KV):
            columns = slice(kv_head * HD, (kv_head + 1) * HD)
            wide_buf[kv_head] = dot_nn(kv[slot, 1, :, columns], g_turned[kv_head])
        for kv_head in range(HALF_KV):
            columns = slice(kv_head * HD, (kv_head + 1) * HD)
            heads = slice(kv_head * GROUP, (kv_head + 1) * GROUP)
            stacked = (GROUP * pair_rows, HD)
            for at in range(0, GROUP * pair_rows, CHUNK):
                lanes = slice(at, at + CHUNK)
                level = (
                    jnp.exp2(msave[slot, kv_head, :, lanes] - m_cur[kv_head, :, lanes])
                    * l_cur[kv_head, :, lanes]
                )
                probability = psave[slot, kv_head, :, lanes].astype(F32) * level
                grad_prob = wide_buf[kv_head, :, lanes]
                grad_score = probability * (grad_prob - row_dot[kv_head, :, lanes])
                p_buf[kv_head, :, lanes] = probability.astype(BF16)
                ds_buf[kv_head, :, lanes] = grad_score.astype(BF16)
            put(1, columns, dot_nn(p_buf[kv_head], gs[heads].reshape(stacked)))
            put(
                0,
                columns,
                dot_nn(ds_buf[kv_head], qs[heads].reshape(stacked)) * scaling,
            )
            dq_acc[kv_head] = dq_acc[kv_head] + dot_nn(
                kv[slot, 0, :, columns].T, ds_buf[kv_head]
            )

    def part_copy(slot, row_core):
        return remote(
            part.at[slot, :, pl.ds(row_core * rows, rows), :],
            part_in.at[spot, core],
            part_send.at[slot, row_core],
            part_recv.at[spot, core],
            at_chip(slot, plane, row_core),
        )

    def part_swap():
        return remote(
            part.at[spot, :, pl.ds(theirs, rows), :],
            part_in.at[spot, core],
            part_send.at[spot, 0],
            part_recv.at[spot, core],
            partner,
        )

    def backward_step(turn, carried):
        slot = window - 1 - turn

        @pl.when((slot < spot) | has_prev)
        def _():
            def put(which, columns, value):
                part[slot, which, :, columns] = value.astype(BF16)

            contribute(slot, put)

            @pl.when(slot != spot)
            def _():
                for row_core in range(2):
                    part_copy(slot, row_core).start()

            @pl.when(slot == spot)
            def _():
                part_swap().start()

        return carried

    lax.fori_loop(0, window, backward_step, 0)

    def part_arrived(slot, which):
        remote(
            part.at[slot, :, pl.ds(0, rows), :],
            part_in.at[slot, which],
            part_send.at[slot, 0],
            part_recv.at[slot, which],
            partner,
        ).wait_recv()

    z_back = remote(z_out, z_in, z_back_sems.at[0], z_back_sems.at[1], at_chip(spot, plane - 1, core))
    z_back_in = remote(z_out, z_in, z_back_sems.at[0], z_back_sems.at[1], partner)

    def gather(slot, carried):
        for which in range(2):
            part_arrived(slot, which)
            totals[which] += part_in[slot, which].astype(F32)
        return carried

    @pl.when(has_prev)
    def _():
        part_arrived(spot, 1 - core)
        totals[core] = part[spot, :, pl.ds(mine, rows), :].astype(F32)
        totals[1 - core] = part_in[spot, 1 - core].astype(F32)
        lax.fori_loop(0, spot, gather, 0)
        z_out[...] = totals[...].astype(BF16)
        z_back.start()

    def put_own(which, columns, value):
        own_part[which, :, columns] = value

    contribute(own, put_own)

    f_out[...] = own_part[:, pl.ds(theirs, rows), :].astype(BF16)
    f_swap = remote(f_out, f_in, fin_send.at[2], fin_recv.at[2], partner)
    f_swap.start()

    for head in range(HALF_Q):
        kv_head, lanes = head_lanes(head)
        dq_all[head] = (dq_acc[kv_head, :, lanes] * scaling).T.astype(BF16)
    dq_swap = remote(
        dq_all.at[:, pl.ds(theirs, rows), :],
        dq_in,
        fin_send.at[1],
        fin_recv.at[1],
        partner,
    )
    dq_swap.start()

    totals[core] = own_part[:, pl.ds(mine, rows), :]
    f_swap.wait_recv()
    totals[1 - core] = f_in[...].astype(F32)
    lax.fori_loop(spot + 1, window, gather, 0)

    o_swap.wait_recv()
    dq_swap.wait_recv()
    for ref, everything, arrived in ((o_ref, o_all, o_in), (dq_ref, dq_all, dq_in)):
        for head in range(HALF_Q):
            here = everything[head, pl.ds(mine, rows), :]
            there = arrived[head]
            ref[:, head * HD : (head + 1) * HD] = jnp.where(low, here, there)
            ref[:, (head + HALF_Q) * HD : (head + HALF_Q + 1) * HD] = jnp.where(
                low, there, here
            )

    @pl.when(has_next)
    def _():
        z_back_in.wait_recv()
        totals[...] += z_in[...].astype(F32)

    for which in range(2):
        half = slice(which * wide, (which + 1) * wide)
        dk_ref[:, half] = totals[which, 0].astype(BF16)
        dv_ref[:, half] = totals[which, 1].astype(BF16)

    for copy in (kv_swap, q_swap, g_swap, o_swap, dq_swap, f_swap):
        copy.wait_send()

    @pl.when(has_next)
    def _():
        for part_of in range(2):
            for which in range(2):
                z_copy(which, part_of).wait_send()

    @pl.when(has_prev)
    def _():
        z_back.wait_send()
        part_swap().wait_send()

    for delta in range(1, window):

        @pl.when(spot + delta < window)
        def _(delta=delta):
            for which in range(2):
                plane_copy(delta, which).wait_send()

        @pl.when((spot + delta >= window) & has_prev)
        def _(delta=delta):
            for part_of in range(2):
                plane_pass(delta, part_of).wait_send()

    def sent(slot, carried):
        @pl.when(((slot < spot) | has_prev) & (slot != spot))
        def _():
            for row_core in range(2):
                part_copy(slot, row_core).wait_send()

        return carried

    lax.fori_loop(0, window, sent, 0)


def hand_over(*refs):
    sems = refs[8]
    copies = []
    for source, target in zip(refs[:4], refs[4:8]):
        rows = source.shape[0]
        step = rows // 2
        for first in range(0, rows, step):
            piece = pl.ds(first, step)
            copy = pltpu.make_async_copy(
                source.at[piece, :], target.at[piece, :], sems.at[len(copies)]
            )
            copy.start()
            copies.append(copy)
    for copy in copies:
        copy.wait()


def per_device(seq, tp, query_rows, key_rows, value_rows, out_grad, doc_lengths):
    rows = query_rows.shape[0]
    pairs = seq * tp // 2
    planes = 4
    window = pairs // planes
    pair_rows = 2 * rows
    wide = HALF_KV * HD
    blocks = window + 1
    long = GROUP * pair_rows
    dma = pltpu.SemaphoreType.DMA
    vmem = pltpu.VMEM
    scratch = [
        vmem((blocks, 2, pair_rows, wide), BF16),
        vmem((HALF_Q, pair_rows, HD), BF16),
        vmem((HALF_Q, pair_rows, HD), BF16),
        vmem((HALF_Q, rows, HD), BF16),
        vmem((HALF_Q, rows, HD), BF16),
        vmem((2, 2, rows, wide), BF16),
        vmem((blocks, HALF_KV, pair_rows, long), BF16),
        vmem((blocks, HALF_KV, 1, long), F32),
        vmem((HALF_KV, 1, long), F32),
        vmem((HALF_KV, 1, long), F32),
        vmem((HALF_KV, 1, long), F32),
        vmem((HALF_KV, HD, long), F32),
        vmem((HALF_KV, 1, long), F32),
        vmem((HALF_KV, HD, long), F32),
        vmem((pair_rows, pair_rows), F32),
        vmem((HALF_KV, HD, long), BF16),
        vmem((HALF_KV, HD, long), BF16),
        vmem((HALF_KV, pair_rows, long), F32),
        vmem((HALF_KV, pair_rows, long), BF16),
        vmem((HALF_KV, pair_rows, long), BF16),
        vmem((window, 2, pair_rows, wide), BF16),
        vmem((window, 2, 2, rows, wide), BF16),
        vmem((2, pair_rows, wide), F32),
        vmem((2, 2, rows, wide), F32),
        vmem((2, 2, rows, wide), BF16),
        vmem((2, 2, rows, wide), BF16),
        vmem((HALF_Q, pair_rows, HD), BF16),
        vmem((HALF_Q, rows, HD), BF16),
        vmem((HALF_Q, pair_rows, HD), BF16),
        vmem((HALF_Q, rows, HD), BF16),
        vmem((2, rows, wide), BF16),
        vmem((2, rows, wide), BF16),
        dma((3,)),
        dma((3,)),
        dma((2, 2)),
        dma((2, 2)),
        dma((2,)),
        dma((window, 2)),
        dma((window, 2)),
        dma((window, 2)),
        dma((window, 2)),
        dma((3,)),
        dma((3,)),
    ]
    whole = pl.BlockSpec(memory_space=pltpu.VMEM)

    def body(*refs):
        kernel(tp, window, planes, *refs)

    shapes = tuple(
        jax.ShapeDtypeStruct(x.shape, BF16)
        for x in (query_rows, query_rows, key_rows, value_rows)
    )
    results = pl.pallas_call(
        body,
        out_shape=shapes,
        in_specs=[whole] * 4 + [pl.BlockSpec(memory_space=pltpu.SMEM)],
        out_specs=(whole,) * 4,
        scratch_shapes=scratch,
        compiler_params=pltpu.CompilerParams(
            collective_id=0,
            has_side_effects=True,
            vmem_limit_bytes=60 * 2**20,
        ),
        name="packed_attention",
    )(query_rows, key_rows, value_rows, out_grad, doc_lengths)
    left = pl.BlockSpec(memory_space=pl.ANY)
    return pl.pallas_call(
        hand_over,
        out_shape=shapes,
        in_specs=[left] * 4,
        out_specs=(left,) * 4,
        scratch_shapes=[dma((8,))],
        name="hand_over",
    )(*results)


def solution(mesh):
    seq, tp = mesh.shape["seq"], mesh.shape["tp"]
    spec = P(("seq", "tp"), None)

    def run(*args):
        return per_device(seq, tp, *args)

    return jax.shard_map(
        run,
        mesh=mesh,
        in_specs=(spec, spec, spec, spec, P()),
        out_specs=(spec,) * 4,
        check_vma=False,
    )
```

```python
import math

import jax
import jax.numpy as jnp
from jax import lax
from jax.experimental import pallas as pl
from jax.experimental.pallas import tpu as pltpu
from jax.sharding import PartitionSpec as P

HD = 128
QH = 20
KVH = 4
GROUP = QH // KVH
HALF_Q = QH // 2
HALF_KV = KVH // 2
CHUNK = 128
MESH = pl.DeviceIdType.MESH
F32 = jnp.float32
BF16 = jnp.bfloat16


def dot_nt(a, b):
    return lax.dot_general(a, b, (((1,), (1,)), ((), ())), preferred_element_type=F32)


def dot_nn(a, b):
    return lax.dot_general(a, b, (((1,), (0,)), ((), ())), preferred_element_type=F32)


def kernel(
    tp,
    window,
    planes,
    q_ref,
    k_ref,
    v_ref,
    g_ref,
    len_ref,
    o_ref,
    dq_ref,
    dk_ref,
    dv_ref,
    kv,
    qs,
    gs,
    q_stage,
    g_stage,
    kv_stage,
    psave,
    msave,
    m_cur,
    l_cur,
    shrinks,
    acc,
    row_dot,
    dq_acc,
    bias,
    q_turned,
    g_turned,
    wide_buf,
    p_buf,
    ds_buf,
    part,
    part_in,
    own_part,
    totals,
    z_out,
    z_in,
    o_all,
    o_in,
    dq_all,
    dq_in,
    f_out,
    f_in,
    ex_send,
    ex_recv,
    z_send,
    z_recv,
    z_back_sems,
    plane_send,
    plane_recv,
    part_send,
    part_recv,
    fin_send,
    fin_recv,
):
    rows = q_ref.shape[0]
    pair_rows = 2 * rows
    wide = HALF_KV * HD
    own = window
    me = lax.axis_index("seq") * tp + lax.axis_index("tp")
    core = me % 2
    pair = me // 2
    plane = pair // window
    spot = pair % window
    has_prev = plane > 0
    has_next = plane < planes - 1
    low = core == 0
    mine = pl.multiple_of(core * rows, rows)
    theirs = pl.multiple_of((1 - core) * rows, rows)

    def device(index):
        return (index // tp, index % tp)

    def at_chip(in_plane, which_plane, which_core):
        return device(2 * (which_plane * window + in_plane) + which_core)

    partner = device(2 * pair + 1 - core)

    def head_lanes(head):
        kv_head, within = divmod(head, GROUP)
        return kv_head, slice(within * pair_rows, (within + 1) * pair_rows)

    def remote(src, dst, send_sem, recv_sem, target):
        return pltpu.make_async_remote_copy(
            src_ref=src,
            dst_ref=dst,
            send_sem=send_sem,
            recv_sem=recv_sem,
            device_id=target,
            device_id_type=MESH,
        )

    barrier = pltpu.get_barrier_semaphore()

    def greet(target):
        pl.semaphore_signal(barrier, inc=1, device_id=target, device_id_type=MESH)

    greet(partner)
    for which in range(2):
        for delta in range(1, window):
            greet(at_chip((spot + delta) % window, plane, which))

        @pl.when(has_prev)
        def _(which=which):
            greet(at_chip(spot, plane - 1, which))

        @pl.when(has_next)
        def _(which=which):
            greet(at_chip(spot, plane + 1, which))

    k_all = k_ref[...]
    v_all = v_ref[...]
    for which in range(2):
        half = slice(which * wide, (which + 1) * wide)
        kv_stage[which, 0] = k_all[:, half]
        kv_stage[which, 1] = v_all[:, half]
    kv[own, 0, pl.ds(mine, rows), :] = jnp.where(low, k_all[:, :wide], k_all[:, wide:])
    kv[own, 1, pl.ds(mine, rows), :] = jnp.where(low, v_all[:, :wide], v_all[:, wide:])

    neighbours = has_prev.astype(jnp.int32) + has_next.astype(jnp.int32)
    pl.semaphore_wait(barrier, 2 * window - 1 + 2 * neighbours)

    def z_copy(which, part_of):
        return remote(
            kv_stage.at[which, part_of],
            kv.at[spot, part_of, pl.ds(mine, rows), :],
            z_send.at[which, part_of],
            z_recv.at[core, part_of],
            at_chip(spot, plane + 1, which),
        )

    def z_arrival(row_core, part_of):
        return remote(
            kv_stage.at[0, part_of],
            kv.at[spot, part_of, pl.ds(row_core * rows, rows), :],
            z_send.at[0, part_of],
            z_recv.at[row_core, part_of],
            partner,
        )

    def plane_copy(delta, which):
        return remote(
            kv_stage.at[which],
            kv.at[spot, :, pl.ds(mine, rows), :],
            plane_send.at[delta, which],
            plane_recv.at[spot, core],
            at_chip((spot + delta) % window, plane, which),
        )

    def plane_pass(delta, part_of):
        return remote(
            kv.at[spot, part_of],
            kv.at[spot, part_of],
            plane_send.at[delta, part_of],
            plane_recv.at[spot, part_of],
            at_chip((spot + delta) % window, plane, core),
        )

    kv_swap = remote(
        kv_stage.at[1 - core],
        kv.at[own, :, pl.ds(mine, rows), :],
        ex_send.at[0],
        ex_recv.at[0],
        partner,
    )
    kv_swap.start()

    @pl.when(has_next)
    def _():
        for part_of in range(2):
            for which in range(2):
                z_copy(which, part_of).start()

    for delta in range(1, window):

        @pl.when(spot + delta < window)
        def _(delta=delta):
            for which in range(2):
                plane_copy(delta, which).start()

    swaps = []
    for index, (stage, held, ref) in enumerate(
        ((q_stage, qs, q_ref), (g_stage, gs, g_ref))
    ):
        for head in range(HALF_Q):
            left = ref[:, head * HD : (head + 1) * HD]
            right = ref[:, (head + HALF_Q) * HD : (head + HALF_Q + 1) * HD]
            stage[head] = jnp.where(low, right, left)
            held[head, pl.ds(mine, rows), :] = jnp.where(low, left, right)
        swap = remote(
            stage,
            held.at[:, pl.ds(mine, rows), :],
            ex_send.at[index + 1],
            ex_recv.at[index + 1],
            partner,
        )
        swap.start()
        swaps.append(swap)
    q_swap, g_swap = swaps

    ends = []
    total = jnp.int32(0)
    for doc in range(len_ref.shape[0]):
        total = total + len_ref[doc]
        ends.append(total)
    query_pos = pair * pair_rows + lax.broadcasted_iota(jnp.int32, (1, pair_rows), 1)
    first_key = jnp.zeros((1, pair_rows), jnp.int32)
    for end in ends:
        first_key = jnp.where(query_pos >= end, end, first_key)

    factor2 = HD ** (-0.5) * math.log2(math.e)
    scaling = HD ** (-0.5)

    def absorb(slot, block, first):
        key_pos = block * pair_rows + lax.broadcasted_iota(
            jnp.int32, (pair_rows, pair_rows), 0
        )
        bias[...] = jnp.where(
            (key_pos <= query_pos) & (key_pos >= first_key), 0.0, -1e30
        )
        for kv_head in range(HALF_KV):
            columns = slice(kv_head * HD, (kv_head + 1) * HD)
            wide_buf[kv_head] = dot_nn(kv[slot, 0, :, columns], q_turned[kv_head])
        for kv_head in range(HALF_KV):
            columns = slice(kv_head * HD, (kv_head + 1) * HD)
            for at in range(0, GROUP * pair_rows, CHUNK):
                lanes = slice(at, at + CHUNK)
                tokens = slice(at % pair_rows, at % pair_rows + CHUNK)
                score = wide_buf[kv_head, :, lanes] * factor2 + bias[:, tokens]
                newest = jnp.max(score, axis=0, keepdims=True)
                if not first:
                    before = m_cur[kv_head, :, lanes]
                    newest = jnp.maximum(before, newest)
                weight = jnp.exp2(score - newest)
                row_sum = jnp.sum(weight, axis=0, keepdims=True)
                psave[slot, kv_head, :, lanes] = weight.astype(BF16)
                msave[slot, kv_head, :, lanes] = newest
                if not first:
                    shrink = jnp.exp2(before - newest)
                    row_sum = l_cur[kv_head, :, lanes] * shrink + row_sum
                    shrinks[kv_head, :, lanes] = shrink
                l_cur[kv_head, :, lanes] = row_sum
                m_cur[kv_head, :, lanes] = newest
            product = dot_nn(kv[slot, 1, :, columns].T, psave[slot, kv_head])
            if first:
                acc[kv_head] = product
            else:
                acc[kv_head] = acc[kv_head] * shrinks[kv_head] + product

    q_swap.wait_recv()
    for head in range(HALF_Q):
        kv_head, lanes = head_lanes(head)
        q_turned[kv_head, :, lanes] = qs[head].T
    kv_swap.wait_recv()
    absorb(own, pair, True)

    @pl.when(has_prev)
    def _():
        for part_of in range(2):
            for row_core in range(2):
                z_arrival(row_core, part_of).wait_recv()
            for delta in range(1, window):

                @pl.when(spot + delta >= window)
                def _(delta=delta, part_of=part_of):
                    plane_pass(delta, part_of).start()

    def forward_step(turn, carried):
        slot = (spot + window - turn) % window

        @pl.when((slot < spot) | has_prev)
        def _():
            @pl.when(slot < spot)
            def _():
                for row_core in range(2):
                    remote(
                        kv_stage.at[0],
                        kv.at[slot, :, pl.ds(row_core * rows, rows), :],
                        plane_send.at[0, row_core],
                        plane_recv.at[slot, row_core],
                        partner,
                    ).wait_recv()

            @pl.when(slot > spot)
            def _():
                for part_of in range(2):
                    remote(
                        kv.at[own, part_of],
                        kv.at[slot, part_of],
                        plane_send.at[0, part_of],
                        plane_recv.at[slot, part_of],
                        partner,
                    ).wait_recv()

            block = jnp.where(slot < spot, plane, plane - 1) * window + slot
            absorb(slot, block, False)

        return carried

    lax.fori_loop(0, window, forward_step, 0)
    g_swap.wait_recv()

    for head in range(HALF_Q):
        kv_head, lanes = head_lanes(head)
        inverse = 1.0 / l_cur[kv_head, :, lanes]
        out_turned = acc[kv_head, :, lanes] * inverse
        o_all[head] = out_turned.T.astype(BF16)
        grad_turned = gs[head].T
        g_turned[kv_head, :, lanes] = grad_turned
        row_dot[kv_head, :, lanes] = jnp.sum(
            grad_turned.astype(F32) * out_turned.astype(BF16).astype(F32),
            axis=0,
            keepdims=True,
        )
        l_cur[kv_head, :, lanes] = inverse
    dq_acc[...] = jnp.zeros_like(dq_acc)

    o_swap = remote(
        o_all.at[:, pl.ds(theirs, rows), :], o_in, fin_send.at[0], fin_recv.at[0], partner
    )
    o_swap.start()

    def contribute(slot, put):
        for kv_head in range(HALF_KV):
            columns = slice(kv_head * HD, (kv_head + 1) * HD)
            wide_buf[kv_head] = dot_nn(kv[slot, 1, :, columns], g_turned[kv_head])
        for kv_head in range(HALF_KV):
            columns = slice(kv_head * HD, (kv_head + 1) * HD)
            heads = slice(kv_head * GROUP, (kv_head + 1) * GROUP)
            stacked = (GROUP * pair_rows, HD)
            for at in range(0, GROUP * pair_rows, CHUNK):
                lanes = slice(at, at + CHUNK)
                level = (
                    jnp.exp2(msave[slot, kv_head, :, lanes] - m_cur[kv_head, :, lanes])
                    * l_cur[kv_head, :, lanes]
                )
                probability = psave[slot, kv_head, :, lanes].astype(F32) * level
                grad_prob = wide_buf[kv_head, :, lanes]
                grad_score = probability * (grad_prob - row_dot[kv_head, :, lanes])
                p_buf[kv_head, :, lanes] = probability.astype(BF16)
                ds_buf[kv_head, :, lanes] = grad_score.astype(BF16)
            put(1, columns, dot_nn(p_buf[kv_head], gs[heads].reshape(stacked)))
            put(
                0,
                columns,
                dot_nn(ds_buf[kv_head], qs[heads].reshape(stacked)) * scaling,
            )
            dq_acc[kv_head] = dq_acc[kv_head] + dot_nn(
                kv[slot, 0, :, columns].T, ds_buf[kv_head]
            )

    def part_copy(slot, row_core):
        return remote(
            part.at[slot, :, pl.ds(row_core * rows, rows), :],
            part_in.at[spot, core],
            part_send.at[slot, row_core],
            part_recv.at[spot, core],
            at_chip(slot, plane, row_core),
        )

    def part_swap():
        return remote(
            part.at[spot, :, pl.ds(theirs, rows), :],
            part_in.at[spot, core],
            part_send.at[spot, 0],
            part_recv.at[spot, core],
            partner,
        )

    def backward_step(turn, carried):
        slot = (spot + window - 1 - turn) % window

        @pl.when((slot < spot) | has_prev)
        def _():
            def put(which, columns, value):
                part[slot, which, :, columns] = value.astype(BF16)

            contribute(slot, put)

            @pl.when(slot != spot)
            def _():
                for row_core in range(2):
                    part_copy(slot, row_core).start()

            @pl.when(slot == spot)
            def _():
                part_swap().start()

        return carried

    lax.fori_loop(0, window, backward_step, 0)

    def part_arrived(slot, which):
        remote(
            part.at[slot, :, pl.ds(0, rows), :],
            part_in.at[slot, which],
            part_send.at[slot, 0],
            part_recv.at[slot, which],
            partner,
        ).wait_recv()

    z_back = remote(z_out, z_in, z_back_sems.at[0], z_back_sems.at[1], at_chip(spot, plane - 1, core))
    z_back_in = remote(z_out, z_in, z_back_sems.at[0], z_back_sems.at[1], partner)

    def gather(slot, carried):
        for which in range(2):
            part_arrived(slot, which)
            totals[which] += part_in[slot, which].astype(F32)
        return carried

    @pl.when(has_prev)
    def _():
        part_arrived(spot, 1 - core)
        totals[core] = part[spot, :, pl.ds(mine, rows), :].astype(F32)
        totals[1 - core] = part_in[spot, 1 - core].astype(F32)
        lax.fori_loop(0, spot, gather, 0)
        z_out[...] = totals[...].astype(BF16)
        z_back.start()

    def put_own(which, columns, value):
        own_part[which, :, columns] = value

    contribute(own, put_own)

    f_out[...] = own_part[:, pl.ds(theirs, rows), :].astype(BF16)
    f_swap = remote(f_out, f_in, fin_send.at[2], fin_recv.at[2], partner)
    f_swap.start()

    for head in range(HALF_Q):
        kv_head, lanes = head_lanes(head)
        dq_all[head] = (dq_acc[kv_head, :, lanes] * scaling).T.astype(BF16)
    dq_swap = remote(
        dq_all.at[:, pl.ds(theirs, rows), :],
        dq_in,
        fin_send.at[1],
        fin_recv.at[1],
        partner,
    )
    dq_swap.start()

    totals[core] = own_part[:, pl.ds(mine, rows), :]
    f_swap.wait_recv()
    totals[1 - core] = f_in[...].astype(F32)
    lax.fori_loop(spot + 1, window, gather, 0)

    o_swap.wait_recv()
    dq_swap.wait_recv()
    for ref, everything, arrived in ((o_ref, o_all, o_in), (dq_ref, dq_all, dq_in)):
        for head in range(HALF_Q):
            here = everything[head, pl.ds(mine, rows), :]
            there = arrived[head]
            ref[:, head * HD : (head + 1) * HD] = jnp.where(low, here, there)
            ref[:, (head + HALF_Q) * HD : (head + HALF_Q + 1) * HD] = jnp.where(
                low, there, here
            )

    @pl.when(has_next)
    def _():
        z_back_in.wait_recv()
        totals[...] += z_in[...].astype(F32)

    for which in range(2):
        half = slice(which * wide, (which + 1) * wide)
        dk_ref[:, half] = totals[which, 0].astype(BF16)
        dv_ref[:, half] = totals[which, 1].astype(BF16)

    for copy in (kv_swap, q_swap, g_swap, o_swap, dq_swap, f_swap):
        copy.wait_send()

    @pl.when(has_next)
    def _():
        for part_of in range(2):
            for which in range(2):
                z_copy(which, part_of).wait_send()

    @pl.when(has_prev)
    def _():
        z_back.wait_send()
        part_swap().wait_send()

    for delta in range(1, window):

        @pl.when(spot + delta < window)
        def _(delta=delta):
            for which in range(2):
                plane_copy(delta, which).wait_send()

        @pl.when((spot + delta >= window) & has_prev)
        def _(delta=delta):
            for part_of in range(2):
                plane_pass(delta, part_of).wait_send()

    def sent(slot, carried):
        @pl.when(((slot < spot) | has_prev) & (slot != spot))
        def _():
            for row_core in range(2):
                part_copy(slot, row_core).wait_send()

        return carried

    lax.fori_loop(0, window, sent, 0)


def hand_over(*refs):
    sources, targets, holds, sems = refs[:4], refs[4:8], refs[8:12], refs[12]
    pieces = []
    for index, source in enumerate(sources):
        rows = source.shape[0]
        cuts = 2 if source.shape[1] > rows * 8 else 1
        for first in range(0, rows, rows // cuts):
            pieces.append((index, pl.ds(first, rows // cuts)))
    inward, outward = [], []
    for at, (index, piece) in enumerate(pieces):
        copy = pltpu.make_async_copy(
            sources[index].at[piece, :], holds[index].at[piece, :], sems.at[0, at]
        )
        copy.start()
        inward.append(copy)
    for at, (index, piece) in enumerate(pieces):
        inward[at].wait()
        copy = pltpu.make_async_copy(
            holds[index].at[piece, :], targets[index].at[piece, :], sems.at[1, at]
        )
        copy.start()
        outward.append(copy)
    for copy in outward:
        copy.wait()


def per_device(seq, tp, query_rows, key_rows, value_rows, out_grad, doc_lengths):
    rows = query_rows.shape[0]
    pairs = seq * tp // 2
    planes = 4
    window = pairs // planes
    pair_rows = 2 * rows
    wide = HALF_KV * HD
    blocks = window + 1
    long = GROUP * pair_rows
    dma = pltpu.SemaphoreType.DMA
    vmem = pltpu.VMEM
    scratch = [
        vmem((blocks, 2, pair_rows, wide), BF16),
        vmem((HALF_Q, pair_rows, HD), BF16),
        vmem((HALF_Q, pair_rows, HD), BF16),
        vmem((HALF_Q, rows, HD), BF16),
        vmem((HALF_Q, rows, HD), BF16),
        vmem((2, 2, rows, wide), BF16),
        vmem((blocks, HALF_KV, pair_rows, long), BF16),
        vmem((blocks, HALF_KV, 1, long), F32),
        vmem((HALF_KV, 1, long), F32),
        vmem((HALF_KV, 1, long), F32),
        vmem((HALF_KV, 1, long), F32),
        vmem((HALF_KV, HD, long), F32),
        vmem((HALF_KV, 1, long), F32),
        vmem((HALF_KV, HD, long), F32),
        vmem((pair_rows, pair_rows), F32),
        vmem((HALF_KV, HD, long), BF16),
        vmem((HALF_KV, HD, long), BF16),
        vmem((HALF_KV, pair_rows, long), F32),
        vmem((HALF_KV, pair_rows, long), BF16),
        vmem((HALF_KV, pair_rows, long), BF16),
        vmem((window, 2, pair_rows, wide), BF16),
        vmem((window, 2, 2, rows, wide), BF16),
        vmem((2, pair_rows, wide), F32),
        vmem((2, 2, rows, wide), F32),
        vmem((2, 2, rows, wide), BF16),
        vmem((2, 2, rows, wide), BF16),
        vmem((HALF_Q, pair_rows, HD), BF16),
        vmem((HALF_Q, rows, HD), BF16),
        vmem((HALF_Q, pair_rows, HD), BF16),
        vmem((HALF_Q, rows, HD), BF16),
        vmem((2, rows, wide), BF16),
        vmem((2, rows, wide), BF16),
        dma((3,)),
        dma((3,)),
        dma((2, 2)),
        dma((2, 2)),
        dma((2,)),
        dma((window, 2)),
        dma((window, 2)),
        dma((window, 2)),
        dma((window, 2)),
        dma((3,)),
        dma((3,)),
    ]
    whole = pl.BlockSpec(memory_space=pltpu.VMEM)

    def body(*refs):
        kernel(tp, window, planes, *refs)

    shapes = tuple(
        jax.ShapeDtypeStruct(x.shape, BF16)
        for x in (query_rows, query_rows, key_rows, value_rows)
    )
    results = pl.pallas_call(
        body,
        out_shape=shapes,
        in_specs=[whole] * 4 + [pl.BlockSpec(memory_space=pltpu.SMEM)],
        out_specs=(whole,) * 4,
        scratch_shapes=scratch,
        compiler_params=pltpu.CompilerParams(
            collective_id=0,
            has_side_effects=True,
            vmem_limit_bytes=60 * 2**20,
        ),
        name="packed_attention",
    )(query_rows, key_rows, value_rows, out_grad, doc_lengths)
    left = pl.BlockSpec(memory_space=pl.ANY)
    return pl.pallas_call(
        hand_over,
        out_shape=shapes,
        in_specs=[left] * 4,
        out_specs=(left,) * 4,
        scratch_shapes=[vmem(x.shape, BF16) for x in shapes] + [dma((2, 8))],
        name="hand_over",
    )(*results)


def solution(mesh):
    seq, tp = mesh.shape["seq"], mesh.shape["tp"]
    spec = P(("seq", "tp"), None)

    def run(*args):
        return per_device(seq, tp, *args)

    return jax.shard_map(
        run,
        mesh=mesh,
        in_specs=(spec, spec, spec, spec, P()),
        out_specs=(spec,) * 4,
        check_vma=False,
    )
```

```python
import math

import jax
import jax.numpy as jnp
from jax import lax
from jax.experimental import pallas as pl
from jax.experimental.pallas import tpu as pltpu
from jax.sharding import PartitionSpec as P

HD = 128
QH = 20
KVH = 4
GROUP = QH // KVH
HALF_Q = QH // 2
HALF_KV = KVH // 2
CHUNK = 128
MESH = pl.DeviceIdType.MESH
F32 = jnp.float32
BF16 = jnp.bfloat16


def dot_nt(a, b):
    return lax.dot_general(a, b, (((1,), (1,)), ((), ())), preferred_element_type=F32)


def dot_nn(a, b):
    return lax.dot_general(a, b, (((1,), (0,)), ((), ())), preferred_element_type=F32)


def kernel(
    tp,
    window,
    planes,
    q_ref,
    k_ref,
    v_ref,
    g_ref,
    len_ref,
    o_ref,
    dq_ref,
    dk_ref,
    dv_ref,
    kv,
    qs,
    gs,
    q_stage,
    g_stage,
    kv_stage,
    psave,
    msave,
    m_cur,
    l_cur,
    shrinks,
    acc,
    row_dot,
    dq_acc,
    bias,
    q_turned,
    g_turned,
    wide_buf,
    p_buf,
    ds_buf,
    part,
    part_in,
    own_part,
    totals,
    z_out,
    z_in,
    o_all,
    o_in,
    dq_all,
    dq_in,
    f_out,
    f_in,
    ex_send,
    ex_recv,
    z_send,
    z_recv,
    z_back_sems,
    plane_send,
    plane_recv,
    part_send,
    part_recv,
    fin_send,
    fin_recv,
):
    rows = q_ref.shape[0]
    pair_rows = 2 * rows
    wide = HALF_KV * HD
    own = window
    me = lax.axis_index("seq") * tp + lax.axis_index("tp")
    core = me % 2
    pair = me // 2
    plane = pair // window
    spot = pair % window
    has_prev = plane > 0
    has_next = plane < planes - 1
    low = core == 0
    mine = pl.multiple_of(core * rows, rows)
    theirs = pl.multiple_of((1 - core) * rows, rows)

    def device(index):
        return (index // tp, index % tp)

    def at_chip(in_plane, which_plane, which_core):
        return device(2 * (which_plane * window + in_plane) + which_core)

    partner = device(2 * pair + 1 - core)

    def head_lanes(head):
        kv_head, within = divmod(head, GROUP)
        return kv_head, slice(within * pair_rows, (within + 1) * pair_rows)

    def remote(src, dst, send_sem, recv_sem, target):
        return pltpu.make_async_remote_copy(
            src_ref=src,
            dst_ref=dst,
            send_sem=send_sem,
            recv_sem=recv_sem,
            device_id=target,
            device_id_type=MESH,
        )

    barrier = pltpu.get_barrier_semaphore()

    def greet(target):
        pl.semaphore_signal(barrier, inc=1, device_id=target, device_id_type=MESH)

    greet(partner)
    for which in range(2):
        for delta in range(1, window):
            greet(at_chip((spot + delta) % window, plane, which))

        @pl.when(has_prev)
        def _(which=which):
            greet(at_chip(spot, plane - 1, which))

        @pl.when(has_next)
        def _(which=which):
            greet(at_chip(spot, plane + 1, which))

    k_all = k_ref[...]
    v_all = v_ref[...]
    for which in range(2):
        half = slice(which * wide, (which + 1) * wide)
        kv_stage[which, 0] = k_all[:, half]
        kv_stage[which, 1] = v_all[:, half]
    kv[own, 0, pl.ds(mine, rows), :] = jnp.where(low, k_all[:, :wide], k_all[:, wide:])
    kv[own, 1, pl.ds(mine, rows), :] = jnp.where(low, v_all[:, :wide], v_all[:, wide:])

    neighbours = has_prev.astype(jnp.int32) + has_next.astype(jnp.int32)
    pl.semaphore_wait(barrier, 2 * window - 1 + 2 * neighbours)

    def z_copy(which, part_of):
        return remote(
            kv_stage.at[which, part_of],
            kv.at[spot, part_of, pl.ds(mine, rows), :],
            z_send.at[which, part_of],
            z_recv.at[core, part_of],
            at_chip(spot, plane + 1, which),
        )

    def z_arrival(row_core, part_of):
        return remote(
            kv_stage.at[0, part_of],
            kv.at[spot, part_of, pl.ds(row_core * rows, rows), :],
            z_send.at[0, part_of],
            z_recv.at[row_core, part_of],
            partner,
        )

    def plane_copy(delta, which):
        return remote(
            kv_stage.at[which],
            kv.at[spot, :, pl.ds(mine, rows), :],
            plane_send.at[delta, which],
            plane_recv.at[spot, core],
            at_chip((spot + delta) % window, plane, which),
        )

    def plane_pass(delta, part_of):
        return remote(
            kv.at[spot, part_of],
            kv.at[spot, part_of],
            plane_send.at[delta, part_of],
            plane_recv.at[spot, part_of],
            at_chip((spot + delta) % window, plane, core),
        )

    kv_swap = remote(
        kv_stage.at[1 - core],
        kv.at[own, :, pl.ds(mine, rows), :],
        ex_send.at[0],
        ex_recv.at[0],
        partner,
    )
    kv_swap.start()

    @pl.when(has_next)
    def _():
        for part_of in range(2):
            for which in range(2):
                z_copy(which, part_of).start()

    for delta in range(1, window):

        @pl.when(spot + delta < window)
        def _(delta=delta):
            for which in range(2):
                plane_copy(delta, which).start()

    swaps = []
    for index, (stage, held, ref) in enumerate(
        ((q_stage, qs, q_ref), (g_stage, gs, g_ref))
    ):
        for head in range(HALF_Q):
            left = ref[:, head * HD : (head + 1) * HD]
            right = ref[:, (head + HALF_Q) * HD : (head + HALF_Q + 1) * HD]
            stage[head] = jnp.where(low, right, left)
            held[head, pl.ds(mine, rows), :] = jnp.where(low, left, right)
        swap = remote(
            stage,
            held.at[:, pl.ds(mine, rows), :],
            ex_send.at[index + 1],
            ex_recv.at[index + 1],
            partner,
        )
        swap.start()
        swaps.append(swap)
    q_swap, g_swap = swaps

    ends = []
    total = jnp.int32(0)
    for doc in range(len_ref.shape[0]):
        total = total + len_ref[doc]
        ends.append(total)
    query_pos = pair * pair_rows + lax.broadcasted_iota(jnp.int32, (1, pair_rows), 1)
    first_key = jnp.zeros((1, pair_rows), jnp.int32)
    for end in ends:
        first_key = jnp.where(query_pos >= end, end, first_key)

    factor2 = HD ** (-0.5) * math.log2(math.e)
    scaling = HD ** (-0.5)

    def absorb(slot, block, first):
        key_pos = block * pair_rows + lax.broadcasted_iota(
            jnp.int32, (pair_rows, pair_rows), 0
        )
        bias[...] = jnp.where(
            (key_pos <= query_pos) & (key_pos >= first_key), 0.0, -1e30
        )
        for kv_head in range(HALF_KV):
            columns = slice(kv_head * HD, (kv_head + 1) * HD)
            wide_buf[kv_head] = dot_nn(kv[slot, 0, :, columns], q_turned[kv_head])
        for kv_head in range(HALF_KV):
            columns = slice(kv_head * HD, (kv_head + 1) * HD)
            for at in range(0, GROUP * pair_rows, CHUNK):
                lanes = slice(at, at + CHUNK)
                tokens = slice(at % pair_rows, at % pair_rows + CHUNK)
                score = wide_buf[kv_head, :, lanes] * factor2 + bias[:, tokens]
                newest = jnp.max(score, axis=0, keepdims=True)
                if not first:
                    before = m_cur[kv_head, :, lanes]
                    newest = jnp.maximum(before, newest)
                weight = jnp.exp2(score - newest)
                row_sum = jnp.sum(weight, axis=0, keepdims=True)
                psave[slot, kv_head, :, lanes] = weight.astype(BF16)
                msave[slot, kv_head, :, lanes] = newest
                if not first:
                    shrink = jnp.exp2(before - newest)
                    row_sum = l_cur[kv_head, :, lanes] * shrink + row_sum
                    shrinks[kv_head, :, lanes] = shrink
                l_cur[kv_head, :, lanes] = row_sum
                m_cur[kv_head, :, lanes] = newest
            product = dot_nn(kv[slot, 1, :, columns].T, psave[slot, kv_head])
            if first:
                acc[kv_head] = product
            else:
                acc[kv_head] = acc[kv_head] * shrinks[kv_head] + product

    q_swap.wait_recv()
    for head in range(HALF_Q):
        kv_head, lanes = head_lanes(head)
        q_turned[kv_head, :, lanes] = qs[head].T
    kv_swap.wait_recv()
    absorb(own, pair, True)

    @pl.when(has_prev)
    def _():
        for part_of in range(2):
            for row_core in range(2):
                z_arrival(row_core, part_of).wait_recv()
            for delta in range(1, window):

                @pl.when(spot + delta >= window)
                def _(delta=delta, part_of=part_of):
                    plane_pass(delta, part_of).start()

    def forward_step(turn, carried):
        slot = (spot + window - turn) % window

        @pl.when((slot < spot) | has_prev)
        def _():
            @pl.when(slot < spot)
            def _():
                for row_core in range(2):
                    remote(
                        kv_stage.at[0],
                        kv.at[slot, :, pl.ds(row_core * rows, rows), :],
                        plane_send.at[0, row_core],
                        plane_recv.at[slot, row_core],
                        partner,
                    ).wait_recv()

            @pl.when(slot > spot)
            def _():
                for part_of in range(2):
                    remote(
                        kv.at[own, part_of],
                        kv.at[slot, part_of],
                        plane_send.at[0, part_of],
                        plane_recv.at[slot, part_of],
                        partner,
                    ).wait_recv()

            block = jnp.where(slot < spot, plane, plane - 1) * window + slot
            absorb(slot, block, False)

        return carried

    lax.fori_loop(0, window, forward_step, 0)
    g_swap.wait_recv()

    for head in range(HALF_Q):
        kv_head, lanes = head_lanes(head)
        inverse = 1.0 / l_cur[kv_head, :, lanes]
        out_turned = acc[kv_head, :, lanes] * inverse
        o_all[head] = out_turned.T.astype(BF16)
        grad_turned = gs[head].T
        g_turned[kv_head, :, lanes] = grad_turned
        row_dot[kv_head, :, lanes] = jnp.sum(
            grad_turned.astype(F32) * out_turned.astype(BF16).astype(F32),
            axis=0,
            keepdims=True,
        )
        l_cur[kv_head, :, lanes] = inverse
    dq_acc[...] = jnp.zeros_like(dq_acc)

    o_swap = remote(
        o_all.at[:, pl.ds(theirs, rows), :], o_in, fin_send.at[0], fin_recv.at[0], partner
    )
    o_swap.start()

    def contribute(slot, put):
        for kv_head in range(HALF_KV):
            columns = slice(kv_head * HD, (kv_head + 1) * HD)
            wide_buf[kv_head] = dot_nn(kv[slot, 1, :, columns], g_turned[kv_head])
        for kv_head in range(HALF_KV):
            columns = slice(kv_head * HD, (kv_head + 1) * HD)
            heads = slice(kv_head * GROUP, (kv_head + 1) * GROUP)
            stacked = (GROUP * pair_rows, HD)
            for at in range(0, GROUP * pair_rows, CHUNK):
                lanes = slice(at, at + CHUNK)
                level = (
                    jnp.exp2(msave[slot, kv_head, :, lanes] - m_cur[kv_head, :, lanes])
                    * l_cur[kv_head, :, lanes]
                )
                probability = psave[slot, kv_head, :, lanes].astype(F32) * level
                grad_prob = wide_buf[kv_head, :, lanes]
                grad_score = probability * (grad_prob - row_dot[kv_head, :, lanes])
                p_buf[kv_head, :, lanes] = probability.astype(BF16)
                ds_buf[kv_head, :, lanes] = grad_score.astype(BF16)
            put(1, columns, dot_nn(p_buf[kv_head], gs[heads].reshape(stacked)))
            put(
                0,
                columns,
                dot_nn(ds_buf[kv_head], qs[heads].reshape(stacked)) * scaling,
            )
            dq_acc[kv_head] = dq_acc[kv_head] + dot_nn(
                kv[slot, 0, :, columns].T, ds_buf[kv_head]
            )

    def part_copy(slot, row_core, part_of):
        return remote(
            part.at[slot, part_of, pl.ds(row_core * rows, rows), :],
            part_in.at[spot, core, part_of],
            part_send.at[slot, row_core, part_of],
            part_recv.at[spot, core, part_of],
            at_chip(slot, plane, row_core),
        )

    def part_swap(part_of):
        return remote(
            part.at[spot, part_of, pl.ds(theirs, rows), :],
            part_in.at[spot, core, part_of],
            part_send.at[spot, 0, part_of],
            part_recv.at[spot, core, part_of],
            partner,
        )

    def backward_step(turn, carried):
        pattern = window - 1 - turn
        slot = 0
        bit = 1
        while bit < window:
            slot = slot + ((spot // bit + pattern // bit) % 2) * bit
            bit *= 2

        @pl.when((slot < spot) | has_prev)
        def _():
            def put(which, columns, value):
                part[slot, which, :, columns] = value.astype(BF16)

            contribute(slot, put)

            @pl.when(slot != spot)
            def _():
                for part_of in range(2):
                    for row_core in range(2):
                        part_copy(slot, row_core, part_of).start()

            @pl.when(slot == spot)
            def _():
                for part_of in range(2):
                    part_swap(part_of).start()

        return carried

    lax.fori_loop(0, window, backward_step, 0)

    def part_arrived(slot, which, part_of):
        remote(
            part.at[slot, part_of, pl.ds(0, rows), :],
            part_in.at[slot, which, part_of],
            part_send.at[slot, 0, part_of],
            part_recv.at[slot, which, part_of],
            partner,
        ).wait_recv()

    def z_back(part_of):
        return remote(
            z_out.at[part_of],
            z_in.at[part_of],
            z_back_sems.at[0, part_of],
            z_back_sems.at[1, part_of],
            at_chip(spot, plane - 1, core),
        )

    def z_back_in(part_of):
        return remote(
            z_out.at[part_of],
            z_in.at[part_of],
            z_back_sems.at[0, part_of],
            z_back_sems.at[1, part_of],
            partner,
        )

    def gather(part_of):
        def step(slot, carried):
            for which in range(2):
                part_arrived(slot, which, part_of)
                totals[part_of, which] += part_in[slot, which, part_of].astype(F32)
            return carried

        return step

    @pl.when(has_prev)
    def _():
        for part_of in range(2):
            part_arrived(spot, 1 - core, part_of)
            totals[part_of, core] = part[spot, part_of, pl.ds(mine, rows), :].astype(F32)
            totals[part_of, 1 - core] = part_in[spot, 1 - core, part_of].astype(F32)
            lax.fori_loop(0, spot, gather(part_of), 0)
            z_out[part_of] = totals[part_of].astype(BF16)
            z_back(part_of).start()

    def put_own(which, columns, value):
        own_part[which, :, columns] = value

    contribute(own, put_own)

    f_out[...] = own_part[:, pl.ds(theirs, rows), :].astype(BF16)
    f_swap = remote(f_out, f_in, fin_send.at[2], fin_recv.at[2], partner)
    f_swap.start()

    for head in range(HALF_Q):
        kv_head, lanes = head_lanes(head)
        dq_all[head] = (dq_acc[kv_head, :, lanes] * scaling).T.astype(BF16)
    dq_swap = remote(
        dq_all.at[:, pl.ds(theirs, rows), :],
        dq_in,
        fin_send.at[1],
        fin_recv.at[1],
        partner,
    )
    dq_swap.start()

    f_swap.wait_recv()
    for part_of in range(2):
        totals[part_of, core] = own_part[part_of, pl.ds(mine, rows), :]
        totals[part_of, 1 - core] = f_in[part_of].astype(F32)
        lax.fori_loop(spot + 1, window, gather(part_of), 0)

    o_swap.wait_recv()
    dq_swap.wait_recv()
    for ref, everything, arrived in ((o_ref, o_all, o_in), (dq_ref, dq_all, dq_in)):
        for head in range(HALF_Q):
            here = everything[head, pl.ds(mine, rows), :]
            there = arrived[head]
            ref[:, head * HD : (head + 1) * HD] = jnp.where(low, here, there)
            ref[:, (head + HALF_Q) * HD : (head + HALF_Q + 1) * HD] = jnp.where(
                low, there, here
            )

    @pl.when(has_next)
    def _():
        for part_of in range(2):
            z_back_in(part_of).wait_recv()
        totals[...] += z_in[...].astype(F32)

    for which in range(2):
        half = slice(which * wide, (which + 1) * wide)
        dk_ref[:, half] = totals[0, which].astype(BF16)
        dv_ref[:, half] = totals[1, which].astype(BF16)

    for copy in (kv_swap, q_swap, g_swap, o_swap, dq_swap, f_swap):
        copy.wait_send()

    @pl.when(has_next)
    def _():
        for part_of in range(2):
            for which in range(2):
                z_copy(which, part_of).wait_send()

    @pl.when(has_prev)
    def _():
        for part_of in range(2):
            z_back(part_of).wait_send()
            part_swap(part_of).wait_send()

    for delta in range(1, window):

        @pl.when(spot + delta < window)
        def _(delta=delta):
            for which in range(2):
                plane_copy(delta, which).wait_send()

        @pl.when((spot + delta >= window) & has_prev)
        def _(delta=delta):
            for part_of in range(2):
                plane_pass(delta, part_of).wait_send()

    def sent(slot, carried):
        @pl.when(((slot < spot) | has_prev) & (slot != spot))
        def _():
            for part_of in range(2):
                for row_core in range(2):
                    part_copy(slot, row_core, part_of).wait_send()

        return carried

    lax.fori_loop(0, window, sent, 0)


def hand_over(*refs):
    sources, targets, holds, sems = refs[:4], refs[4:8], refs[8:12], refs[12]
    pieces = []
    for index, source in enumerate(sources):
        rows = source.shape[0]
        cuts = 2 if source.shape[1] > rows * 8 else 1
        for first in range(0, rows, rows // cuts):
            pieces.append((index, pl.ds(first, rows // cuts)))
    inward, outward = [], []
    for at, (index, piece) in enumerate(pieces):
        copy = pltpu.make_async_copy(
            sources[index].at[piece, :], holds[index].at[piece, :], sems.at[0, at]
        )
        copy.start()
        inward.append(copy)
    for at, (index, piece) in enumerate(pieces):
        inward[at].wait()
        copy = pltpu.make_async_copy(
            holds[index].at[piece, :], targets[index].at[piece, :], sems.at[1, at]
        )
        copy.start()
        outward.append(copy)
    for copy in outward:
        copy.wait()


def per_device(seq, tp, query_rows, key_rows, value_rows, out_grad, doc_lengths):
    rows = query_rows.shape[0]
    pairs = seq * tp // 2
    planes = 4
    window = pairs // planes
    pair_rows = 2 * rows
    wide = HALF_KV * HD
    blocks = window + 1
    long = GROUP * pair_rows
    dma = pltpu.SemaphoreType.DMA
    vmem = pltpu.VMEM
    scratch = [
        vmem((blocks, 2, pair_rows, wide), BF16),
        vmem((HALF_Q, pair_rows, HD), BF16),
        vmem((HALF_Q, pair_rows, HD), BF16),
        vmem((HALF_Q, rows, HD), BF16),
        vmem((HALF_Q, rows, HD), BF16),
        vmem((2, 2, rows, wide), BF16),
        vmem((blocks, HALF_KV, pair_rows, long), BF16),
        vmem((blocks, HALF_KV, 1, long), F32),
        vmem((HALF_KV, 1, long), F32),
        vmem((HALF_KV, 1, long), F32),
        vmem((HALF_KV, 1, long), F32),
        vmem((HALF_KV, HD, long), F32),
        vmem((HALF_KV, 1, long), F32),
        vmem((HALF_KV, HD, long), F32),
        vmem((pair_rows, pair_rows), F32),
        vmem((HALF_KV, HD, long), BF16),
        vmem((HALF_KV, HD, long), BF16),
        vmem((HALF_KV, pair_rows, long), F32),
        vmem((HALF_KV, pair_rows, long), BF16),
        vmem((HALF_KV, pair_rows, long), BF16),
        vmem((window, 2, pair_rows, wide), BF16),
        vmem((window, 2, 2, rows, wide), BF16),
        vmem((2, pair_rows, wide), F32),
        vmem((2, 2, rows, wide), F32),
        vmem((2, 2, rows, wide), BF16),
        vmem((2, 2, rows, wide), BF16),
        vmem((HALF_Q, pair_rows, HD), BF16),
        vmem((HALF_Q, rows, HD), BF16),
        vmem((HALF_Q, pair_rows, HD), BF16),
        vmem((HALF_Q, rows, HD), BF16),
        vmem((2, rows, wide), BF16),
        vmem((2, rows, wide), BF16),
        dma((3,)),
        dma((3,)),
        dma((2, 2)),
        dma((2, 2)),
        dma((2, 2)),
        dma((window, 2)),
        dma((window, 2)),
        dma((window, 2, 2)),
        dma((window, 2, 2)),
        dma((3,)),
        dma((3,)),
    ]
    whole = pl.BlockSpec(memory_space=pltpu.VMEM)

    def body(*refs):
        kernel(tp, window, planes, *refs)

    shapes = tuple(
        jax.ShapeDtypeStruct(x.shape, BF16)
        for x in (query_rows, query_rows, key_rows, value_rows)
    )
    results = pl.pallas_call(
        body,
        out_shape=shapes,
        in_specs=[whole] * 4 + [pl.BlockSpec(memory_space=pltpu.SMEM)],
        out_specs=(whole,) * 4,
        scratch_shapes=scratch,
        compiler_params=pltpu.CompilerParams(
            collective_id=0,
            has_side_effects=True,
            vmem_limit_bytes=60 * 2**20,
        ),
        name="packed_attention",
    )(query_rows, key_rows, value_rows, out_grad, doc_lengths)
    left = pl.BlockSpec(memory_space=pl.ANY)
    return pl.pallas_call(
        hand_over,
        out_shape=shapes,
        in_specs=[left] * 4,
        out_specs=(left,) * 4,
        scratch_shapes=[vmem(x.shape, BF16) for x in shapes] + [dma((2, 8))],
        name="hand_over",
    )(*results)


def solution(mesh):
    seq, tp = mesh.shape["seq"], mesh.shape["tp"]
    spec = P(("seq", "tp"), None)

    def run(*args):
        return per_device(seq, tp, *args)

    return jax.shard_map(
        run,
        mesh=mesh,
        in_specs=(spec, spec, spec, spec, P()),
        out_specs=(spec,) * 4,
        check_vma=False,
    )
```

```python
import math

import jax
import jax.numpy as jnp
from jax import lax
from jax.experimental import pallas as pl
from jax.experimental.pallas import tpu as pltpu
from jax.sharding import PartitionSpec as P

HD = 128
QH = 20
KVH = 4
GROUP = QH // KVH
HALF_Q = QH // 2
HALF_KV = KVH // 2
CHUNK = 128
MESH = pl.DeviceIdType.MESH
F32 = jnp.float32
BF16 = jnp.bfloat16


def dot_nt(a, b):
    return lax.dot_general(a, b, (((1,), (1,)), ((), ())), preferred_element_type=F32)


def dot_nn(a, b):
    return lax.dot_general(a, b, (((1,), (0,)), ((), ())), preferred_element_type=F32)


def kernel(
    tp,
    window,
    planes,
    q_hbm,
    k_ref,
    v_ref,
    g_hbm,
    len_ref,
    o_hbm,
    dq_hbm,
    dk_ref,
    dv_ref,
    kv,
    qs,
    gs,
    q_stage,
    g_stage,
    kv_stage,
    psave,
    msave,
    m_cur,
    l_cur,
    shrinks,
    acc,
    row_dot,
    dq_acc,
    bias,
    q_turned,
    g_turned,
    wide_buf,
    p_buf,
    ds_buf,
    part,
    part_in,
    own_part,
    totals,
    z_out,
    z_in,
    o_all,
    o_in,
    dq_all,
    dq_in,
    f_out,
    f_in,
    ex_send,
    ex_recv,
    z_send,
    z_recv,
    z_back_sems,
    plane_send,
    plane_recv,
    part_send,
    part_recv,
    fin_send,
    fin_recv,
    q_ref,
    g_ref,
    o_ref,
    dq_ref,
    local_sems,
):
    q_fetch = pltpu.make_async_copy(q_hbm, q_ref, local_sems.at[0])
    g_fetch = pltpu.make_async_copy(g_hbm, g_ref, local_sems.at[1])
    q_fetch.start()
    g_fetch.start()
    rows = q_ref.shape[0]
    pair_rows = 2 * rows
    wide = HALF_KV * HD
    own = window
    me = lax.axis_index("seq") * tp + lax.axis_index("tp")
    core = me % 2
    pair = me // 2
    plane = pair // window
    spot = pair % window
    has_prev = plane > 0
    has_next = plane < planes - 1
    low = core == 0
    mine = pl.multiple_of(core * rows, rows)
    theirs = pl.multiple_of((1 - core) * rows, rows)

    def device(index):
        return (index // tp, index % tp)

    def at_chip(in_plane, which_plane, which_core):
        return device(2 * (which_plane * window + in_plane) + which_core)

    partner = device(2 * pair + 1 - core)

    def head_lanes(head):
        kv_head, within = divmod(head, GROUP)
        return kv_head, slice(within * pair_rows, (within + 1) * pair_rows)

    def remote(src, dst, send_sem, recv_sem, target):
        return pltpu.make_async_remote_copy(
            src_ref=src,
            dst_ref=dst,
            send_sem=send_sem,
            recv_sem=recv_sem,
            device_id=target,
            device_id_type=MESH,
        )

    barrier = pltpu.get_barrier_semaphore()

    def greet(target):
        pl.semaphore_signal(barrier, inc=1, device_id=target, device_id_type=MESH)

    greet(partner)
    for which in range(2):
        for delta in range(1, window):
            greet(at_chip((spot + delta) % window, plane, which))

        @pl.when(has_prev)
        def _(which=which):
            greet(at_chip(spot, plane - 1, which))

        @pl.when(has_next)
        def _(which=which):
            greet(at_chip(spot, plane + 1, which))

    k_all = k_ref[...]
    v_all = v_ref[...]
    for which in range(2):
        half = slice(which * wide, (which + 1) * wide)
        kv_stage[which, 0] = k_all[:, half]
        kv_stage[which, 1] = v_all[:, half]
    kv[own, 0, pl.ds(mine, rows), :] = jnp.where(low, k_all[:, :wide], k_all[:, wide:])
    kv[own, 1, pl.ds(mine, rows), :] = jnp.where(low, v_all[:, :wide], v_all[:, wide:])

    neighbours = has_prev.astype(jnp.int32) + has_next.astype(jnp.int32)
    pl.semaphore_wait(barrier, 2 * window - 1 + 2 * neighbours)

    def z_copy(which, part_of):
        return remote(
            kv_stage.at[which, part_of],
            kv.at[spot, part_of, pl.ds(mine, rows), :],
            z_send.at[which, part_of],
            z_recv.at[core, part_of],
            at_chip(spot, plane + 1, which),
        )

    def z_arrival(row_core, part_of):
        return remote(
            kv_stage.at[0, part_of],
            kv.at[spot, part_of, pl.ds(row_core * rows, rows), :],
            z_send.at[0, part_of],
            z_recv.at[row_core, part_of],
            partner,
        )

    def plane_copy(delta, which):
        return remote(
            kv_stage.at[which],
            kv.at[spot, :, pl.ds(mine, rows), :],
            plane_send.at[delta, which],
            plane_recv.at[spot, core],
            at_chip((spot + delta) % window, plane, which),
        )

    def plane_pass(delta, part_of):
        return remote(
            kv.at[spot, part_of],
            kv.at[spot, part_of],
            plane_send.at[delta, part_of],
            plane_recv.at[spot, part_of],
            at_chip((spot + delta) % window, plane, core),
        )

    kv_swap = remote(
        kv_stage.at[1 - core],
        kv.at[own, :, pl.ds(mine, rows), :],
        ex_send.at[0],
        ex_recv.at[0],
        partner,
    )
    kv_swap.start()

    @pl.when(has_next)
    def _():
        for part_of in range(2):
            for which in range(2):
                z_copy(which, part_of).start()

    for delta in range(1, window):

        @pl.when(spot + delta < window)
        def _(delta=delta):
            for which in range(2):
                plane_copy(delta, which).start()

    swaps = []
    for index, (stage, held, ref, fetch) in enumerate(
        ((q_stage, qs, q_ref, q_fetch), (g_stage, gs, g_ref, g_fetch))
    ):
        fetch.wait()
        for head in range(HALF_Q):
            left = ref[:, head * HD : (head + 1) * HD]
            right = ref[:, (head + HALF_Q) * HD : (head + HALF_Q + 1) * HD]
            stage[head] = jnp.where(low, right, left)
            held[head, pl.ds(mine, rows), :] = jnp.where(low, left, right)
        swap = remote(
            stage,
            held.at[:, pl.ds(mine, rows), :],
            ex_send.at[index + 1],
            ex_recv.at[index + 1],
            partner,
        )
        swap.start()
        swaps.append(swap)
    q_swap, g_swap = swaps

    ends = []
    total = jnp.int32(0)
    for doc in range(len_ref.shape[0]):
        total = total + len_ref[doc]
        ends.append(total)
    query_pos = pair * pair_rows + lax.broadcasted_iota(jnp.int32, (1, pair_rows), 1)
    first_key = jnp.zeros((1, pair_rows), jnp.int32)
    for end in ends:
        first_key = jnp.where(query_pos >= end, end, first_key)

    factor2 = HD ** (-0.5) * math.log2(math.e)
    scaling = HD ** (-0.5)

    def absorb(slot, block, first):
        key_pos = block * pair_rows + lax.broadcasted_iota(
            jnp.int32, (pair_rows, pair_rows), 0
        )
        bias[...] = jnp.where(
            (key_pos <= query_pos) & (key_pos >= first_key), 0.0, -1e30
        )
        for kv_head in range(HALF_KV):
            columns = slice(kv_head * HD, (kv_head + 1) * HD)
            wide_buf[kv_head] = dot_nn(kv[slot, 0, :, columns], q_turned[kv_head])
        for kv_head in range(HALF_KV):
            columns = slice(kv_head * HD, (kv_head + 1) * HD)
            for at in range(0, GROUP * pair_rows, CHUNK):
                lanes = slice(at, at + CHUNK)
                tokens = slice(at % pair_rows, at % pair_rows + CHUNK)
                score = wide_buf[kv_head, :, lanes] * factor2 + bias[:, tokens]
                newest = jnp.max(score, axis=0, keepdims=True)
                if not first:
                    before = m_cur[kv_head, :, lanes]
                    newest = jnp.maximum(before, newest)
                weight = jnp.exp2(score - newest)
                row_sum = jnp.sum(weight, axis=0, keepdims=True)
                psave[slot, kv_head, :, lanes] = weight.astype(BF16)
                msave[slot, kv_head, :, lanes] = newest
                if not first:
                    shrink = jnp.exp2(before - newest)
                    row_sum = l_cur[kv_head, :, lanes] * shrink + row_sum
                    shrinks[kv_head, :, lanes] = shrink
                l_cur[kv_head, :, lanes] = row_sum
                m_cur[kv_head, :, lanes] = newest
            product = dot_nn(kv[slot, 1, :, columns].T, psave[slot, kv_head])
            if first:
                acc[kv_head] = product
            else:
                acc[kv_head] = acc[kv_head] * shrinks[kv_head] + product

    q_swap.wait_recv()
    for head in range(HALF_Q):
        kv_head, lanes = head_lanes(head)
        q_turned[kv_head, :, lanes] = qs[head].T
    kv_swap.wait_recv()
    absorb(own, pair, True)

    @pl.when(has_prev)
    def _():
        for part_of in range(2):
            for row_core in range(2):
                z_arrival(row_core, part_of).wait_recv()
            for delta in range(1, window):

                @pl.when(spot + delta >= window)
                def _(delta=delta, part_of=part_of):
                    plane_pass(delta, part_of).start()

    def forward_step(turn, carried):
        slot = (spot + window - turn) % window

        @pl.when((slot < spot) | has_prev)
        def _():
            @pl.when(slot < spot)
            def _():
                for row_core in range(2):
                    remote(
                        kv_stage.at[0],
                        kv.at[slot, :, pl.ds(row_core * rows, rows), :],
                        plane_send.at[0, row_core],
                        plane_recv.at[slot, row_core],
                        partner,
                    ).wait_recv()

            @pl.when(slot > spot)
            def _():
                for part_of in range(2):
                    remote(
                        kv.at[own, part_of],
                        kv.at[slot, part_of],
                        plane_send.at[0, part_of],
                        plane_recv.at[slot, part_of],
                        partner,
                    ).wait_recv()

            block = jnp.where(slot < spot, plane, plane - 1) * window + slot
            absorb(slot, block, False)

        return carried

    lax.fori_loop(0, window, forward_step, 0)
    g_swap.wait_recv()

    for head in range(HALF_Q):
        kv_head, lanes = head_lanes(head)
        inverse = 1.0 / l_cur[kv_head, :, lanes]
        out_turned = acc[kv_head, :, lanes] * inverse
        o_all[head] = out_turned.T.astype(BF16)
        grad_turned = gs[head].T
        g_turned[kv_head, :, lanes] = grad_turned
        row_dot[kv_head, :, lanes] = jnp.sum(
            grad_turned.astype(F32) * out_turned.astype(BF16).astype(F32),
            axis=0,
            keepdims=True,
        )
        l_cur[kv_head, :, lanes] = inverse
    dq_acc[...] = jnp.zeros_like(dq_acc)

    o_swap = remote(
        o_all.at[:, pl.ds(theirs, rows), :], o_in, fin_send.at[0], fin_recv.at[0], partner
    )
    o_swap.start()

    def contribute(slot, put, kv_heads=tuple(range(HALF_KV))):
        for kv_head in kv_heads:
            columns = slice(kv_head * HD, (kv_head + 1) * HD)
            wide_buf[kv_head] = dot_nn(kv[slot, 1, :, columns], g_turned[kv_head])
        for kv_head in kv_heads:
            columns = slice(kv_head * HD, (kv_head + 1) * HD)
            heads = slice(kv_head * GROUP, (kv_head + 1) * GROUP)
            stacked = (GROUP * pair_rows, HD)
            for at in range(0, GROUP * pair_rows, CHUNK):
                lanes = slice(at, at + CHUNK)
                level = (
                    jnp.exp2(msave[slot, kv_head, :, lanes] - m_cur[kv_head, :, lanes])
                    * l_cur[kv_head, :, lanes]
                )
                probability = psave[slot, kv_head, :, lanes].astype(F32) * level
                grad_prob = wide_buf[kv_head, :, lanes]
                grad_score = probability * (grad_prob - row_dot[kv_head, :, lanes])
                p_buf[kv_head, :, lanes] = probability.astype(BF16)
                ds_buf[kv_head, :, lanes] = grad_score.astype(BF16)
            put(1, columns, dot_nn(p_buf[kv_head], gs[heads].reshape(stacked)))
            put(
                0,
                columns,
                dot_nn(ds_buf[kv_head], qs[heads].reshape(stacked)) * scaling,
            )
            dq_acc[kv_head] = dq_acc[kv_head] + dot_nn(
                kv[slot, 0, :, columns].T, ds_buf[kv_head]
            )

    def part_copy(slot, row_core, part_of):
        return remote(
            part.at[slot, part_of, pl.ds(row_core * rows, rows), :],
            part_in.at[spot, core, part_of],
            part_send.at[slot, row_core, part_of],
            part_recv.at[spot, core, part_of],
            at_chip(slot, plane, row_core),
        )

    def part_swap(part_of):
        return remote(
            part.at[spot, part_of, pl.ds(theirs, rows), :],
            part_in.at[spot, core, part_of],
            part_send.at[spot, 0, part_of],
            part_recv.at[spot, core, part_of],
            partner,
        )

    def backward_step(turn, carried):
        pattern = window - 1 - turn
        slot = 0
        bit = 1
        while bit < window:
            slot = slot + ((spot // bit + pattern // bit) % 2) * bit
            bit *= 2

        @pl.when((slot < spot) | has_prev)
        def _():
            def put(which, columns, value):
                part[slot, which, :, columns] = value.astype(BF16)

            contribute(slot, put)

            @pl.when(slot != spot)
            def _():
                for part_of in range(2):
                    for row_core in range(2):
                        part_copy(slot, row_core, part_of).start()

            @pl.when(slot == spot)
            def _():
                for part_of in range(2):
                    part_swap(part_of).start()

        return carried

    lax.fori_loop(0, window, backward_step, 0)

    def part_arrived(slot, which, part_of):
        remote(
            part.at[slot, part_of, pl.ds(0, rows), :],
            part_in.at[slot, which, part_of],
            part_send.at[slot, 0, part_of],
            part_recv.at[slot, which, part_of],
            partner,
        ).wait_recv()

    def z_back(part_of):
        return remote(
            z_out.at[part_of],
            z_in.at[part_of],
            z_back_sems.at[0, part_of],
            z_back_sems.at[1, part_of],
            at_chip(spot, plane - 1, core),
        )

    def z_back_in(part_of):
        return remote(
            z_out.at[part_of],
            z_in.at[part_of],
            z_back_sems.at[0, part_of],
            z_back_sems.at[1, part_of],
            partner,
        )

    def gather(part_of):
        def step(slot, carried):
            for which in range(2):
                part_arrived(slot, which, part_of)
                totals[part_of, which] += part_in[slot, which, part_of].astype(F32)
            return carried

        return step

    def put_own(which, columns, value):
        own_part[which, :, columns] = value

    contribute(own, put_own, (0,))

    @pl.when(has_prev)
    def _():
        for part_of in range(2):
            part_arrived(spot, 1 - core, part_of)
            totals[part_of, core] = part[spot, part_of, pl.ds(mine, rows), :].astype(F32)
            totals[part_of, 1 - core] = part_in[spot, 1 - core, part_of].astype(F32)
            lax.fori_loop(0, spot, gather(part_of), 0)
            z_out[part_of] = totals[part_of].astype(BF16)
            z_back(part_of).start()

    contribute(own, put_own, (1,))

    f_out[...] = own_part[:, pl.ds(theirs, rows), :].astype(BF16)
    f_swap = remote(f_out, f_in, fin_send.at[2], fin_recv.at[2], partner)
    f_swap.start()

    for head in range(HALF_Q):
        kv_head, lanes = head_lanes(head)
        dq_all[head] = (dq_acc[kv_head, :, lanes] * scaling).T.astype(BF16)
    dq_swap = remote(
        dq_all.at[:, pl.ds(theirs, rows), :],
        dq_in,
        fin_send.at[1],
        fin_recv.at[1],
        partner,
    )
    dq_swap.start()

    f_swap.wait_recv()
    for part_of in range(2):
        totals[part_of, core] = own_part[part_of, pl.ds(mine, rows), :]
        totals[part_of, 1 - core] = f_in[part_of].astype(F32)
        lax.fori_loop(spot + 1, window, gather(part_of), 0)

    o_swap.wait_recv()
    dq_swap.wait_recv()
    writes = []
    for ref, everything, arrived, target in (
        (o_ref, o_all, o_in, o_hbm),
        (dq_ref, dq_all, dq_in, dq_hbm),
    ):
        for head in range(HALF_Q):
            here = everything[head, pl.ds(mine, rows), :]
            there = arrived[head]
            ref[:, head * HD : (head + 1) * HD] = jnp.where(low, here, there)
            ref[:, (head + HALF_Q) * HD : (head + HALF_Q + 1) * HD] = jnp.where(
                low, there, here
            )
        write = pltpu.make_async_copy(ref, target, local_sems.at[2 + len(writes)])
        write.start()
        writes.append(write)

    @pl.when(has_next)
    def _():
        for part_of in range(2):
            z_back_in(part_of).wait_recv()
        totals[...] += z_in[...].astype(F32)

    for which in range(2):
        half = slice(which * wide, (which + 1) * wide)
        dk_ref[:, half] = totals[0, which].astype(BF16)
        dv_ref[:, half] = totals[1, which].astype(BF16)

    for write in writes:
        write.wait()
    for copy in (kv_swap, q_swap, g_swap, o_swap, dq_swap, f_swap):
        copy.wait_send()

    @pl.when(has_next)
    def _():
        for part_of in range(2):
            for which in range(2):
                z_copy(which, part_of).wait_send()

    @pl.when(has_prev)
    def _():
        for part_of in range(2):
            z_back(part_of).wait_send()
            part_swap(part_of).wait_send()

    for delta in range(1, window):

        @pl.when(spot + delta < window)
        def _(delta=delta):
            for which in range(2):
                plane_copy(delta, which).wait_send()

        @pl.when((spot + delta >= window) & has_prev)
        def _(delta=delta):
            for part_of in range(2):
                plane_pass(delta, part_of).wait_send()

    def sent(slot, carried):
        @pl.when(((slot < spot) | has_prev) & (slot != spot))
        def _():
            for part_of in range(2):
                for row_core in range(2):
                    part_copy(slot, row_core, part_of).wait_send()

        return carried

    lax.fori_loop(0, window, sent, 0)


def hand_over(*refs):
    sources, targets, holds, sems = refs[:4], refs[4:8], refs[8:12], refs[12]
    pieces = []
    for index, source in enumerate(sources):
        rows = source.shape[0]
        cuts = 2 if source.shape[1] > rows * 8 else 1
        for first in range(0, rows, rows // cuts):
            pieces.append((index, pl.ds(first, rows // cuts)))
    inward, outward = [], []
    for at, (index, piece) in enumerate(pieces):
        copy = pltpu.make_async_copy(
            sources[index].at[piece, :], holds[index].at[piece, :], sems.at[0, at]
        )
        copy.start()
        inward.append(copy)
    for at, (index, piece) in enumerate(pieces):
        inward[at].wait()
        copy = pltpu.make_async_copy(
            holds[index].at[piece, :], targets[index].at[piece, :], sems.at[1, at]
        )
        copy.start()
        outward.append(copy)
    for copy in outward:
        copy.wait()


def per_device(seq, tp, query_rows, key_rows, value_rows, out_grad, doc_lengths):
    rows = query_rows.shape[0]
    pairs = seq * tp // 2
    planes = 4
    window = pairs // planes
    pair_rows = 2 * rows
    wide = HALF_KV * HD
    blocks = window + 1
    long = GROUP * pair_rows
    dma = pltpu.SemaphoreType.DMA
    vmem = pltpu.VMEM
    scratch = [
        vmem((blocks, 2, pair_rows, wide), BF16),
        vmem((HALF_Q, pair_rows, HD), BF16),
        vmem((HALF_Q, pair_rows, HD), BF16),
        vmem((HALF_Q, rows, HD), BF16),
        vmem((HALF_Q, rows, HD), BF16),
        vmem((2, 2, rows, wide), BF16),
        vmem((blocks, HALF_KV, pair_rows, long), BF16),
        vmem((blocks, HALF_KV, 1, long), F32),
        vmem((HALF_KV, 1, long), F32),
        vmem((HALF_KV, 1, long), F32),
        vmem((HALF_KV, 1, long), F32),
        vmem((HALF_KV, HD, long), F32),
        vmem((HALF_KV, 1, long), F32),
        vmem((HALF_KV, HD, long), F32),
        vmem((pair_rows, pair_rows), F32),
        vmem((HALF_KV, HD, long), BF16),
        vmem((HALF_KV, HD, long), BF16),
        vmem((HALF_KV, pair_rows, long), F32),
        vmem((HALF_KV, pair_rows, long), BF16),
        vmem((HALF_KV, pair_rows, long), BF16),
        vmem((window, 2, pair_rows, wide), BF16),
        vmem((window, 2, 2, rows, wide), BF16),
        vmem((2, pair_rows, wide), F32),
        vmem((2, 2, rows, wide), F32),
        vmem((2, 2, rows, wide), BF16),
        vmem((2, 2, rows, wide), BF16),
        vmem((HALF_Q, pair_rows, HD), BF16),
        vmem((HALF_Q, rows, HD), BF16),
        vmem((HALF_Q, pair_rows, HD), BF16),
        vmem((HALF_Q, rows, HD), BF16),
        vmem((2, rows, wide), BF16),
        vmem((2, rows, wide), BF16),
        dma((3,)),
        dma((3,)),
        dma((2, 2)),
        dma((2, 2)),
        dma((2, 2)),
        dma((window, 2)),
        dma((window, 2)),
        dma((window, 2, 2)),
        dma((window, 2, 2)),
        dma((3,)),
        dma((3,)),
        vmem((rows, QH * HD), BF16),
        vmem((rows, QH * HD), BF16),
        vmem((rows, QH * HD), BF16),
        vmem((rows, QH * HD), BF16),
        dma((4,)),
    ]
    whole = pl.BlockSpec(memory_space=pltpu.VMEM)
    left = pl.BlockSpec(memory_space=pl.ANY)

    def body(*refs):
        kernel(tp, window, planes, *refs)

    shapes = tuple(
        jax.ShapeDtypeStruct(x.shape, BF16)
        for x in (query_rows, query_rows, key_rows, value_rows)
    )
    results = pl.pallas_call(
        body,
        out_shape=shapes,
        in_specs=[left, whole, whole, left, pl.BlockSpec(memory_space=pltpu.SMEM)],
        out_specs=(left, left, whole, whole),
        scratch_shapes=scratch,
        compiler_params=pltpu.CompilerParams(
            collective_id=0,
            has_side_effects=True,
            vmem_limit_bytes=60 * 2**20,
        ),
        name="packed_attention",
    )(query_rows, key_rows, value_rows, out_grad, doc_lengths)
    return pl.pallas_call(
        hand_over,
        out_shape=shapes,
        in_specs=[left] * 4,
        out_specs=(left,) * 4,
        scratch_shapes=[vmem(x.shape, BF16) for x in shapes] + [dma((2, 8))],
        name="hand_over",
    )(*results)


def solution(mesh):
    seq, tp = mesh.shape["seq"], mesh.shape["tp"]
    spec = P(("seq", "tp"), None)

    def run(*args):
        return per_device(seq, tp, *args)

    return jax.shard_map(
        run,
        mesh=mesh,
        in_specs=(spec, spec, spec, spec, P()),
        out_specs=(spec,) * 4,
        check_vma=False,
    )
```

```python
import math

import jax
import jax.numpy as jnp
from jax import lax
from jax.experimental import pallas as pl
from jax.experimental.pallas import tpu as pltpu
from jax.sharding import PartitionSpec as P

HD = 128
QH = 20
KVH = 4
GROUP = QH // KVH
HALF_Q = QH // 2
HALF_KV = KVH // 2
CHUNK = 128
MESH = pl.DeviceIdType.MESH
F32 = jnp.float32
BF16 = jnp.bfloat16


def dot_nt(a, b):
    return lax.dot_general(a, b, (((1,), (1,)), ((), ())), preferred_element_type=F32)


def dot_nn(a, b):
    return lax.dot_general(a, b, (((1,), (0,)), ((), ())), preferred_element_type=F32)


def kernel(
    tp,
    window,
    planes,
    q_hbm,
    k_ref,
    v_ref,
    g_hbm,
    len_ref,
    o_hbm,
    dq_hbm,
    dk_ref,
    dv_ref,
    kv,
    qs,
    gs,
    q_stage,
    g_stage,
    kv_stage,
    psave,
    msave,
    m_cur,
    l_cur,
    shrinks,
    acc,
    row_dot,
    dq_acc,
    bias,
    q_turned,
    g_turned,
    wide_buf,
    p_buf,
    ds_buf,
    part,
    part_in,
    own_part,
    totals,
    z_out,
    z_in,
    o_all,
    o_in,
    dq_all,
    dq_in,
    f_out,
    f_in,
    ex_send,
    ex_recv,
    z_send,
    z_recv,
    z_back_sems,
    plane_send,
    plane_recv,
    part_send,
    part_recv,
    fin_send,
    fin_recv,
    q_ref,
    g_ref,
    o_ref,
    dq_ref,
    local_sems,
):
    q_fetch = pltpu.make_async_copy(q_hbm, q_ref, local_sems.at[0])
    g_fetch = pltpu.make_async_copy(g_hbm, g_ref, local_sems.at[1])
    q_fetch.start()
    g_fetch.start()
    rows = q_ref.shape[0]
    pair_rows = 2 * rows
    wide = HALF_KV * HD
    own = window
    me = lax.axis_index("seq") * tp + lax.axis_index("tp")
    core = me % 2
    pair = me // 2
    plane = pair // window
    spot = pair % window
    has_prev = plane > 0
    has_next = plane < planes - 1
    low = core == 0
    mine = pl.multiple_of(core * rows, rows)
    theirs = pl.multiple_of((1 - core) * rows, rows)

    def device(index):
        return (index // tp, index % tp)

    def at_chip(in_plane, which_plane, which_core):
        return device(2 * (which_plane * window + in_plane) + which_core)

    partner = device(2 * pair + 1 - core)

    def head_lanes(head):
        kv_head, within = divmod(head, GROUP)
        return kv_head, slice(within * pair_rows, (within + 1) * pair_rows)

    def remote(src, dst, send_sem, recv_sem, target):
        return pltpu.make_async_remote_copy(
            src_ref=src,
            dst_ref=dst,
            send_sem=send_sem,
            recv_sem=recv_sem,
            device_id=target,
            device_id_type=MESH,
        )

    barrier = pltpu.get_barrier_semaphore()

    def greet(target):
        pl.semaphore_signal(barrier, inc=1, device_id=target, device_id_type=MESH)

    greet(partner)
    for which in range(2):
        for delta in range(1, window):
            greet(at_chip((spot + delta) % window, plane, which))

        @pl.when(has_prev)
        def _(which=which):
            greet(at_chip(spot, plane - 1, which))

        @pl.when(has_next)
        def _(which=which):
            greet(at_chip(spot, plane + 1, which))

    k_all = k_ref[...]
    v_all = v_ref[...]
    for which in range(2):
        half = slice(which * wide, (which + 1) * wide)
        kv_stage[which, 0] = k_all[:, half]
        kv_stage[which, 1] = v_all[:, half]
    kv[own, 0, pl.ds(mine, rows), :] = jnp.where(low, k_all[:, :wide], k_all[:, wide:])
    kv[own, 1, pl.ds(mine, rows), :] = jnp.where(low, v_all[:, :wide], v_all[:, wide:])

    neighbours = has_prev.astype(jnp.int32) + has_next.astype(jnp.int32)
    pl.semaphore_wait(barrier, 2 * window - 1 + 2 * neighbours)

    def z_copy(which, part_of):
        return remote(
            kv_stage.at[which, part_of],
            kv.at[spot, part_of, pl.ds(mine, rows), :],
            z_send.at[which, part_of],
            z_recv.at[core, part_of],
            at_chip(spot, plane + 1, which),
        )

    def z_arrival(row_core, part_of):
        return remote(
            kv_stage.at[0, part_of],
            kv.at[spot, part_of, pl.ds(row_core * rows, rows), :],
            z_send.at[0, part_of],
            z_recv.at[row_core, part_of],
            partner,
        )

    def plane_copy(delta, which):
        return remote(
            kv_stage.at[which],
            kv.at[spot, :, pl.ds(mine, rows), :],
            plane_send.at[delta, which],
            plane_recv.at[spot, core],
            at_chip((spot + delta) % window, plane, which),
        )

    def plane_pass(delta, part_of):
        return remote(
            kv.at[spot, part_of],
            kv.at[spot, part_of],
            plane_send.at[delta, part_of],
            plane_recv.at[spot, part_of],
            at_chip((spot + delta) % window, plane, core),
        )

    kv_swap = remote(
        kv_stage.at[1 - core],
        kv.at[own, :, pl.ds(mine, rows), :],
        ex_send.at[0],
        ex_recv.at[0],
        partner,
    )
    kv_swap.start()

    @pl.when(has_next)
    def _():
        for part_of in range(2):
            for which in range(2):
                z_copy(which, part_of).start()

    for delta in range(1, window):

        @pl.when(spot + delta < window)
        def _(delta=delta):
            for which in range(2):
                plane_copy(delta, which).start()

    swaps = []
    for index, (stage, held, ref, fetch) in enumerate(
        ((q_stage, qs, q_ref, q_fetch), (g_stage, gs, g_ref, g_fetch))
    ):
        fetch.wait()
        for head in range(HALF_Q):
            left = ref[:, head * HD : (head + 1) * HD]
            right = ref[:, (head + HALF_Q) * HD : (head + HALF_Q + 1) * HD]
            stage[head] = jnp.where(low, right, left)
            held[head, pl.ds(mine, rows), :] = jnp.where(low, left, right)
        swap = remote(
            stage,
            held.at[:, pl.ds(mine, rows), :],
            ex_send.at[index + 1],
            ex_recv.at[index + 1],
            partner,
        )
        swap.start()
        swaps.append(swap)
    q_swap, g_swap = swaps

    ends = []
    total = jnp.int32(0)
    for doc in range(len_ref.shape[0]):
        total = total + len_ref[doc]
        ends.append(total)
    query_pos = pair * pair_rows + lax.broadcasted_iota(jnp.int32, (1, pair_rows), 1)
    first_key = jnp.zeros((1, pair_rows), jnp.int32)
    for end in ends:
        first_key = jnp.where(query_pos >= end, end, first_key)

    factor2 = HD ** (-0.5) * math.log2(math.e)
    scaling = HD ** (-0.5)

    def absorb(slot, block, first):
        key_pos = block * pair_rows + lax.broadcasted_iota(
            jnp.int32, (pair_rows, pair_rows), 0
        )
        bias[...] = jnp.where(
            (key_pos <= query_pos) & (key_pos >= first_key), 0.0, -1e30
        )
        for kv_head in range(HALF_KV):
            columns = slice(kv_head * HD, (kv_head + 1) * HD)
            wide_buf[kv_head] = dot_nn(kv[slot, 0, :, columns], q_turned[kv_head])
        for kv_head in range(HALF_KV):
            columns = slice(kv_head * HD, (kv_head + 1) * HD)
            for at in range(0, GROUP * pair_rows, CHUNK):
                lanes = slice(at, at + CHUNK)
                tokens = slice(at % pair_rows, at % pair_rows + CHUNK)
                score = wide_buf[kv_head, :, lanes] * factor2 + bias[:, tokens]
                newest = jnp.max(score, axis=0, keepdims=True)
                if not first:
                    before = m_cur[kv_head, :, lanes]
                    newest = jnp.maximum(before, newest)
                weight = jnp.exp2(score - newest)
                row_sum = jnp.sum(weight, axis=0, keepdims=True)
                psave[slot, kv_head, :, lanes] = weight.astype(BF16)
                msave[slot, kv_head, :, lanes] = newest
                if not first:
                    shrink = jnp.exp2(before - newest)
                    row_sum = l_cur[kv_head, :, lanes] * shrink + row_sum
                    shrinks[kv_head, :, lanes] = shrink
                l_cur[kv_head, :, lanes] = row_sum
                m_cur[kv_head, :, lanes] = newest
            product = dot_nn(kv[slot, 1, :, columns].T, psave[slot, kv_head])
            if first:
                acc[kv_head] = product
            else:
                acc[kv_head] = acc[kv_head] * shrinks[kv_head] + product

    q_swap.wait_recv()
    for head in range(HALF_Q):
        kv_head, lanes = head_lanes(head)
        q_turned[kv_head, :, lanes] = qs[head].T
    kv_swap.wait_recv()
    absorb(own, pair, True)

    @pl.when(has_prev)
    def _():
        for part_of in range(2):
            for row_core in range(2):
                z_arrival(row_core, part_of).wait_recv()
            for delta in range(1, window):

                @pl.when(spot + delta >= window)
                def _(delta=delta, part_of=part_of):
                    plane_pass(delta, part_of).start()

    def forward_step(turn, carried):
        slot = (spot + window - turn) % window

        @pl.when((slot < spot) | has_prev)
        def _():
            @pl.when(slot < spot)
            def _():
                for row_core in range(2):
                    remote(
                        kv_stage.at[0],
                        kv.at[slot, :, pl.ds(row_core * rows, rows), :],
                        plane_send.at[0, row_core],
                        plane_recv.at[slot, row_core],
                        partner,
                    ).wait_recv()

            @pl.when(slot > spot)
            def _():
                for part_of in range(2):
                    remote(
                        kv.at[own, part_of],
                        kv.at[slot, part_of],
                        plane_send.at[0, part_of],
                        plane_recv.at[slot, part_of],
                        partner,
                    ).wait_recv()

            block = jnp.where(slot < spot, plane, plane - 1) * window + slot
            absorb(slot, block, False)

        return carried

    lax.fori_loop(0, window, forward_step, 0)
    g_swap.wait_recv()

    for head in range(HALF_Q):
        kv_head, lanes = head_lanes(head)
        inverse = 1.0 / l_cur[kv_head, :, lanes]
        out_turned = acc[kv_head, :, lanes] * inverse
        o_all[head] = out_turned.T.astype(BF16)
        grad_turned = gs[head].T
        g_turned[kv_head, :, lanes] = grad_turned
        row_dot[kv_head, :, lanes] = jnp.sum(
            grad_turned.astype(F32) * out_turned.astype(BF16).astype(F32),
            axis=0,
            keepdims=True,
        )
        l_cur[kv_head, :, lanes] = inverse
    dq_acc[...] = jnp.zeros_like(dq_acc)

    o_swap = remote(
        o_all.at[:, pl.ds(theirs, rows), :], o_in, fin_send.at[0], fin_recv.at[0], partner
    )
    o_swap.start()

    def contribute(slot, put, kv_heads=tuple(range(HALF_KV))):
        for kv_head in kv_heads:
            columns = slice(kv_head * HD, (kv_head + 1) * HD)
            wide_buf[kv_head] = dot_nn(kv[slot, 1, :, columns], g_turned[kv_head])
        for kv_head in kv_heads:
            columns = slice(kv_head * HD, (kv_head + 1) * HD)
            heads = slice(kv_head * GROUP, (kv_head + 1) * GROUP)
            stacked = (GROUP * pair_rows, HD)
            for at in range(0, GROUP * pair_rows, CHUNK):
                lanes = slice(at, at + CHUNK)
                level = (
                    jnp.exp2(msave[slot, kv_head, :, lanes] - m_cur[kv_head, :, lanes])
                    * l_cur[kv_head, :, lanes]
                )
                probability = psave[slot, kv_head, :, lanes].astype(F32) * level
                grad_prob = wide_buf[kv_head, :, lanes]
                grad_score = probability * (grad_prob - row_dot[kv_head, :, lanes])
                p_buf[kv_head, :, lanes] = probability.astype(BF16)
                ds_buf[kv_head, :, lanes] = grad_score.astype(BF16)
            put(1, columns, dot_nn(p_buf[kv_head], gs[heads].reshape(stacked)))
            put(
                0,
                columns,
                dot_nn(ds_buf[kv_head], qs[heads].reshape(stacked)) * scaling,
            )
            dq_acc[kv_head] = dq_acc[kv_head] + dot_nn(
                kv[slot, 0, :, columns].T, ds_buf[kv_head]
            )

    def part_copy(slot, row_core, part_of):
        return remote(
            part.at[slot, part_of, pl.ds(row_core * rows, rows), :],
            part_in.at[spot, core, part_of],
            part_send.at[slot, row_core, part_of],
            part_recv.at[spot, core, part_of],
            at_chip(slot, plane, row_core),
        )

    def part_swap(part_of):
        return remote(
            part.at[spot, part_of, pl.ds(theirs, rows), :],
            part_in.at[spot, core, part_of],
            part_send.at[spot, 0, part_of],
            part_recv.at[spot, core, part_of],
            partner,
        )

    def backward_step(turn, carried):
        pattern = window - 1 - turn
        slot = 0
        bit = 1
        while bit < window:
            slot = slot + ((spot // bit + pattern // bit) % 2) * bit
            bit *= 2

        @pl.when((slot < spot) | has_prev)
        def _():
            def put(which, columns, value):
                part[slot, which, :, columns] = value.astype(BF16)

            contribute(slot, put)

            @pl.when(slot != spot)
            def _():
                for part_of in range(2):
                    for row_core in range(2):
                        part_copy(slot, row_core, part_of).start()

            @pl.when(slot == spot)
            def _():
                for part_of in range(2):
                    part_swap(part_of).start()

        return carried

    lax.fori_loop(0, window, backward_step, 0)

    def part_arrived(slot, which, part_of):
        remote(
            part.at[slot, part_of, pl.ds(0, rows), :],
            part_in.at[slot, which, part_of],
            part_send.at[slot, 0, part_of],
            part_recv.at[slot, which, part_of],
            partner,
        ).wait_recv()

    def z_back(part_of):
        return remote(
            z_out.at[part_of],
            z_in.at[part_of],
            z_back_sems.at[0, part_of],
            z_back_sems.at[1, part_of],
            at_chip(spot, plane - 1, core),
        )

    def z_back_in(part_of):
        return remote(
            z_out.at[part_of],
            z_in.at[part_of],
            z_back_sems.at[0, part_of],
            z_back_sems.at[1, part_of],
            partner,
        )

    def gather(part_of):
        def step(slot, carried):
            for which in range(2):
                part_arrived(slot, which, part_of)
                totals[part_of, which] += part_in[slot, which, part_of].astype(F32)
            return carried

        return step

    def put_own(which, columns, value):
        own_part[which, :, columns] = value

    writes = []

    def deliver(ref, everything, arrived, target):
        for head in range(HALF_Q):
            here = everything[head, pl.ds(mine, rows), :]
            there = arrived[head]
            ref[:, head * HD : (head + 1) * HD] = jnp.where(low, here, there)
            ref[:, (head + HALF_Q) * HD : (head + HALF_Q + 1) * HD] = jnp.where(
                low, there, here
            )
        write = pltpu.make_async_copy(ref, target, local_sems.at[2 + len(writes)])
        write.start()
        writes.append(write)

    def turn_back(kv_head):
        for head in range(kv_head * GROUP, (kv_head + 1) * GROUP):
            lanes = head_lanes(head)[1]
            dq_all[head] = (dq_acc[kv_head, :, lanes] * scaling).T.astype(BF16)

    contribute(own, put_own, (0,))
    turn_back(0)
    o_swap.wait_recv()
    deliver(o_ref, o_all, o_in, o_hbm)

    @pl.when(has_prev)
    def _():
        for part_of in range(2):
            part_arrived(spot, 1 - core, part_of)
            totals[part_of, core] = part[spot, part_of, pl.ds(mine, rows), :].astype(F32)
            totals[part_of, 1 - core] = part_in[spot, 1 - core, part_of].astype(F32)
            lax.fori_loop(0, spot, gather(part_of), 0)
            z_out[part_of] = totals[part_of].astype(BF16)
            z_back(part_of).start()

    contribute(own, put_own, (1,))

    f_out[...] = own_part[:, pl.ds(theirs, rows), :].astype(BF16)
    f_swap = remote(f_out, f_in, fin_send.at[2], fin_recv.at[2], partner)
    f_swap.start()

    turn_back(1)
    dq_swap = remote(
        dq_all.at[:, pl.ds(theirs, rows), :],
        dq_in,
        fin_send.at[1],
        fin_recv.at[1],
        partner,
    )
    dq_swap.start()

    f_swap.wait_recv()
    for part_of in range(2):
        totals[part_of, core] = own_part[part_of, pl.ds(mine, rows), :]
        totals[part_of, 1 - core] = f_in[part_of].astype(F32)
        lax.fori_loop(spot + 1, window, gather(part_of), 0)

    dq_swap.wait_recv()
    deliver(dq_ref, dq_all, dq_in, dq_hbm)

    @pl.when(has_next)
    def _():
        for part_of in range(2):
            z_back_in(part_of).wait_recv()
        totals[...] += z_in[...].astype(F32)

    for which in range(2):
        half = slice(which * wide, (which + 1) * wide)
        dk_ref[:, half] = totals[0, which].astype(BF16)
        dv_ref[:, half] = totals[1, which].astype(BF16)

    for write in writes:
        write.wait()
    for copy in (kv_swap, q_swap, g_swap, o_swap, dq_swap, f_swap):
        copy.wait_send()

    @pl.when(has_next)
    def _():
        for part_of in range(2):
            for which in range(2):
                z_copy(which, part_of).wait_send()

    @pl.when(has_prev)
    def _():
        for part_of in range(2):
            z_back(part_of).wait_send()
            part_swap(part_of).wait_send()

    for delta in range(1, window):

        @pl.when(spot + delta < window)
        def _(delta=delta):
            for which in range(2):
                plane_copy(delta, which).wait_send()

        @pl.when((spot + delta >= window) & has_prev)
        def _(delta=delta):
            for part_of in range(2):
                plane_pass(delta, part_of).wait_send()

    def sent(slot, carried):
        @pl.when(((slot < spot) | has_prev) & (slot != spot))
        def _():
            for part_of in range(2):
                for row_core in range(2):
                    part_copy(slot, row_core, part_of).wait_send()

        return carried

    lax.fori_loop(0, window, sent, 0)


def hand_over(*refs):
    sources, targets, holds, sems = refs[:4], refs[4:8], refs[8:12], refs[12]
    pieces = []
    for index, source in enumerate(sources):
        rows = source.shape[0]
        cuts = 2 if source.shape[1] > rows * 8 else 1
        for first in range(0, rows, rows // cuts):
            pieces.append((index, pl.ds(first, rows // cuts)))
    inward, outward = [], []
    for at, (index, piece) in enumerate(pieces):
        copy = pltpu.make_async_copy(
            sources[index].at[piece, :], holds[index].at[piece, :], sems.at[0, at]
        )
        copy.start()
        inward.append(copy)
    for at, (index, piece) in enumerate(pieces):
        inward[at].wait()
        copy = pltpu.make_async_copy(
            holds[index].at[piece, :], targets[index].at[piece, :], sems.at[1, at]
        )
        copy.start()
        outward.append(copy)
    for copy in outward:
        copy.wait()


def per_device(seq, tp, query_rows, key_rows, value_rows, out_grad, doc_lengths):
    rows = query_rows.shape[0]
    pairs = seq * tp // 2
    planes = 4
    window = pairs // planes
    pair_rows = 2 * rows
    wide = HALF_KV * HD
    blocks = window + 1
    long = GROUP * pair_rows
    dma = pltpu.SemaphoreType.DMA
    vmem = pltpu.VMEM
    scratch = [
        vmem((blocks, 2, pair_rows, wide), BF16),
        vmem((HALF_Q, pair_rows, HD), BF16),
        vmem((HALF_Q, pair_rows, HD), BF16),
        vmem((HALF_Q, rows, HD), BF16),
        vmem((HALF_Q, rows, HD), BF16),
        vmem((2, 2, rows, wide), BF16),
        vmem((blocks, HALF_KV, pair_rows, long), BF16),
        vmem((blocks, HALF_KV, 1, long), F32),
        vmem((HALF_KV, 1, long), F32),
        vmem((HALF_KV, 1, long), F32),
        vmem((HALF_KV, 1, long), F32),
        vmem((HALF_KV, HD, long), F32),
        vmem((HALF_KV, 1, long), F32),
        vmem((HALF_KV, HD, long), F32),
        vmem((pair_rows, pair_rows), F32),
        vmem((HALF_KV, HD, long), BF16),
        vmem((HALF_KV, HD, long), BF16),
        vmem((HALF_KV, pair_rows, long), F32),
        vmem((HALF_KV, pair_rows, long), BF16),
        vmem((HALF_KV, pair_rows, long), BF16),
        vmem((window, 2, pair_rows, wide), BF16),
        vmem((window, 2, 2, rows, wide), BF16),
        vmem((2, pair_rows, wide), F32),
        vmem((2, 2, rows, wide), F32),
        vmem((2, 2, rows, wide), BF16),
        vmem((2, 2, rows, wide), BF16),
        vmem((HALF_Q, pair_rows, HD), BF16),
        vmem((HALF_Q, rows, HD), BF16),
        vmem((HALF_Q, pair_rows, HD), BF16),
        vmem((HALF_Q, rows, HD), BF16),
        vmem((2, rows, wide), BF16),
        vmem((2, rows, wide), BF16),
        dma((3,)),
        dma((3,)),
        dma((2, 2)),
        dma((2, 2)),
        dma((2, 2)),
        dma((window, 2)),
        dma((window, 2)),
        dma((window, 2, 2)),
        dma((window, 2, 2)),
        dma((3,)),
        dma((3,)),
        vmem((rows, QH * HD), BF16),
        vmem((rows, QH * HD), BF16),
        vmem((rows, QH * HD), BF16),
        vmem((rows, QH * HD), BF16),
        dma((4,)),
    ]
    whole = pl.BlockSpec(memory_space=pltpu.VMEM)
    left = pl.BlockSpec(memory_space=pl.ANY)

    def body(*refs):
        kernel(tp, window, planes, *refs)

    shapes = tuple(
        jax.ShapeDtypeStruct(x.shape, BF16)
        for x in (query_rows, query_rows, key_rows, value_rows)
    )
    results = pl.pallas_call(
        body,
        out_shape=shapes,
        in_specs=[left, whole, whole, left, pl.BlockSpec(memory_space=pltpu.SMEM)],
        out_specs=(left, left, whole, whole),
        scratch_shapes=scratch,
        compiler_params=pltpu.CompilerParams(
            collective_id=0,
            has_side_effects=True,
            vmem_limit_bytes=60 * 2**20,
        ),
        name="packed_attention",
    )(query_rows, key_rows, value_rows, out_grad, doc_lengths)
    return pl.pallas_call(
        hand_over,
        out_shape=shapes,
        in_specs=[left] * 4,
        out_specs=(left,) * 4,
        scratch_shapes=[vmem(x.shape, BF16) for x in shapes] + [dma((2, 8))],
        name="hand_over",
    )(*results)


def solution(mesh):
    seq, tp = mesh.shape["seq"], mesh.shape["tp"]
    spec = P(("seq", "tp"), None)

    def run(*args):
        return per_device(seq, tp, *args)

    return jax.shard_map(
        run,
        mesh=mesh,
        in_specs=(spec, spec, spec, spec, P()),
        out_specs=(spec,) * 4,
        check_vma=False,
    )
```
